128 devices in a mesh: stream: 8 (over y_hi, z), girth: 16 (over x, y_lo, core).
Axes of the slice: x: 4, y: 4 (y_hi: 2, y_lo: 2; y = y_hi * 2 + y_lo), z: 4, core: 2. Of those that a mesh axis runs over, the one named last changes fastest.
Arguments:
- velocity: float32 [3, 32, 128, 256], P(None, 'stream', 'girth'), may hold values from -6 to 6
- pressure: float32 [32, 128, 256], P('stream', 'girth'), may hold values from -6 to 6
- kinetic_energy: float32 [32, 128, 256], P('stream', 'girth'), may hold values from 0.01 to 1
- dissipation_rate: float32 [32, 128, 256], P('stream', 'girth'), may hold values from 0.5 to 20
- corner_ids: int32 [128, 1024], replicated, may hold values from 0 to 63230, as said below
- fractions: float32 [3, 128, 1024], replicated, may hold values from 0 to 1
- sector_owner: int32 [64, 1], replicated, may hold values from 0 to 15; in each aligned block of 64 rows (0 to 63, 64 to 127, ...) at most 12 rows name the same one
Outputs:
- new_velocity: float32 [3, 32, 128, 256], P(None, 'stream', 'girth')
- new_energy: float32 [32, 128, 256], P('stream', 'girth')
- new_rate: float32 [32, 128, 256], P('stream', 'girth')
- harmonics: float32 [128, 768], P(('stream', 'girth'))
The draws below stay inside these ranges and needn't reach their ends.
Inputs may be any that keep to these rules, and one draw needn't show every extreme that they name: `corner_ids`: each entry is s * 8 * 256 + g * 256 + q with s from 0 to 30, g from 0 to 6 and q from 0 to 254. `sector_owner`: sector s covers azimuths s * 16 to (s + 1) * 16 - 1. Every girth index owns at least one sector and at most 12, and some girth index owns exactly 12.
All inputs are finite; a program needn't handle non-finite values.
Results may differ from the reference program's by a relative error of at most 0.000076.
Values sent between devices are 32-bit elements; how exact they have to be, the bound alone decides.
A program may use at most 192 MiB of HBM per device.

```python
import math
import jax
import jax.numpy as jnp
import numpy as np
from jax import lax

CG = 8
NR = 256
NRAD = 128
NAZ = 1024
NH = 128
NSEC = 64
NS = 32
NG = 128
SW = 16
MAXSEC = 12
N_GIRTH = 16


def draw_corner_ids(key, part):
    key = jax.random.fold_in(key, 7)
    stream_key, girth_key, radial_key = jax.random.split(key, 3)
    stream_cell = jax.random.randint(stream_key, (NRAD, NAZ), 0, NS - 1)
    girth_cell = jax.random.randint(girth_key, (NRAD, NAZ), 0, CG - 1)
    radial_cell = jax.random.randint(radial_key, (NRAD, NAZ), 0, NR - 1)
    cell_ids = stream_cell * (CG * NR) + girth_cell * NR + radial_cell
    flat_index = lax.broadcasted_iota(jnp.int32, (NRAD, NAZ), 0) * NAZ + lax.broadcasted_iota(jnp.int32, (NRAD, NAZ), 1)
    cell_ids = jnp.where(flat_index == 0, 0, cell_ids)
    cell_ids = jnp.where(flat_index == NRAD * NAZ - 1, (NS - 2) * CG * NR + (CG - 2) * NR + NR - 2, cell_ids)
    return cell_ids.astype(jnp.int32)


def shard_levels(own_key, shape, cuts, smallest, largest):
    def one(dim, blocks):
        draws = jax.random.uniform(jax.random.fold_in(jax.random.fold_in(own_key, 6), dim), (blocks,), jnp.float32, smallest / len(cuts), largest / len(cuts))
        return jnp.repeat(jnp.exp(draws), shape[dim] // blocks).reshape((-1,) + (1,) * (len(shape) - dim - 1))

    loudness = one(*cuts[0])
    for cut in cuts[1:]:
        loudness = loudness * one(*cut)
    return loudness


def assign_block(key, own, number, rows, count, top, bound, slope):
    sequence = jax.random.permutation(key, count)
    crowded, ordinary = load_shares(count, rows * top, bound, slope, True), load_shares(count, rows * top, bound, slope, False)
    places = jnp.arange(count)

    def named(sizes, turn):
        used = int((sizes > 0).sum())
        fixed = max(1, used // 4)
        moved = fixed + (places - fixed + turn * (used - fixed)) % max(1, count - fixed)
        return jnp.zeros((count,), jnp.int32).at[sequence[jnp.where(places < fixed, places, moved)]].set(jnp.asarray(sizes, jnp.int32))

    sizes = jnp.where(number % 4 == 0, named(crowded, number // 4), named(ordinary, number - number // 4 - 1))
    mixed = jax.random.permutation(jax.random.fold_in(own, 3), count)
    source_of, taker = mixed[0:count // 2 * 2:2], mixed[1:count // 2 * 2:2]
    slack = jnp.minimum(sizes[source_of] - 1, bound - sizes[taker]) // 2
    slack = jnp.where((source_of == sequence[0]) | (taker == sequence[0]) | (sizes[taker] == 0), 0, jnp.maximum(slack, 0))
    moved = jax.random.randint(jax.random.fold_in(own, 4), (count // 2,), 0, 1 << 20) % (slack + 1)
    sizes = sizes.at[source_of].add(-moved).at[taker].add(moved)
    labels = jnp.searchsorted(jnp.cumsum(sizes), jnp.arange(rows * top), side="right").astype(jnp.int32)
    table = labels.reshape(top, rows).T
    table = table[jax.random.permutation(jax.random.fold_in(own, 1), rows)]
    turn = jax.random.randint(jax.random.fold_in(own, 2), (rows, 1), 0, top)
    return jnp.take_along_axis(table, (jnp.arange(top)[None, :] + turn) % top, axis=1)


def load_shares(count, total, bound, slope, full):
    loads = [(1 << 20) // math.isqrt(grade ** slope) + 1 for grade in range(1, count + 1)]
    largest = bound if full else min(bound, max(-(-total // count), total * loads[0] // sum(loads)))
    least = 1 if total - largest >= count - 1 else 0
    counts, spare = [largest] + [least] * (count - 1), total - largest - least * (count - 1)
    while spare > 0:
        free = [i for i in range(1, count) if counts[i] < largest] or [i for i in range(1, count) if counts[i] < bound]
        whole, budget = sum([loads[i] for i in free]), spare
        for i in free:
            extra = min(bound - counts[i], max(1, budget * loads[i] // whole), spare)
            counts[i] = counts[i] + extra
            spare = spare - extra
    return np.array(counts)


def bell_draw(own_key, dims, deviation, reach, cuts=(), dtype=jnp.bfloat16):
    drawn = jax.random.normal(own_key, dims, jnp.float32) * deviation
    if len(cuts) > 0:
        drawn = shard_levels(own_key, dims, cuts, -0.22, 0.18) * drawn
    return jnp.clip(drawn, min=-reach, max=reach).astype(dtype)


def setup_inputs(seed: int = 0) -> dict:
    keys = jax.random.split(jax.random.key(seed), 8)
    velocity = bell_draw(keys[0], (3, NS, NG, NR), 1.0, 6.0, ((1, 8), (2, 16)), jnp.float32)
    pressure = bell_draw(keys[1], (NS, NG, NR), 1.0, 6.0, ((0, 8), (1, 16)), jnp.float32)
    kinetic_energy = jnp.clip(jnp.exp(math.log(1.0) - 4.6051702 * jax.random.uniform(keys[2], (NS, NG, NR), jnp.float32) ** shard_levels(keys[2], (NS, NG, NR), ((0, 8), (1, 16)), -0.2, 0.2)), 0.01, 1.0)
    dissipation_rate = jnp.clip(jnp.exp(math.log(20.0) - 3.6888795 * jax.random.uniform(keys[3], (NS, NG, NR), jnp.float32) ** shard_levels(keys[3], (NS, NG, NR), ((0, 8), (1, 16)), -0.2, 0.2)), 0.5, 20.0)
    corner_ids = draw_corner_ids(jax.random.fold_in(keys[7], 71), 0)
    fractions = jnp.clip(jax.random.uniform(keys[5], (3, NRAD, NAZ), jnp.float32, 0.0, 1.0), 0.0, 1.0)
    sector_owner_keys = jax.random.split(jax.random.fold_in(keys[6], 1), NSEC // NSEC)
    sector_owner_turns = jax.random.permutation(jax.random.fold_in(keys[6], 3), NSEC // NSEC)
    sector_owner = jax.vmap(lambda own, number: assign_block(jax.random.fold_in(keys[6], 2), own, number, NSEC, N_GIRTH, 1, MAXSEC, 2))(sector_owner_keys, sector_owner_turns).reshape((NSEC, 1))
    return dict(velocity=velocity, pressure=pressure, kinetic_energy=kinetic_energy, dissipation_rate=dissipation_rate, corner_ids=corner_ids, fractions=fractions, sector_owner=sector_owner)


base_viscosity = 0.05
time_step = 0.2
beta_star = 0.09
beta_rate = 0.075
alpha_rate = 0.52
wall_rate = 1.0


def shifted(values, offsets):
    extent = values.shape
    return values[2 + offsets[0]:extent[0] - 2 + offsets[0], 2 + offsets[1]:extent[1] - 2 + offsets[1], 2 + offsets[2]:extent[2] - 2 + offsets[2]]


def offset_of(direction, amount):
    offsets = [0, 0, 0]
    offsets[direction] = amount
    return tuple(offsets)


def derivative(values, direction):
    near_pair = shifted(values, offset_of(direction, 1)) - shifted(values, offset_of(direction, -1))
    far_pair = shifted(values, offset_of(direction, 2)) - shifted(values, offset_of(direction, -2))
    return (8.0 * near_pair - far_pair) / 12.0


def diffusion(values, viscosity, direction):
    center = shifted(values, (0, 0, 0))
    middle = shifted(viscosity, (0, 0, 0))
    upper_face = 0.5 * (middle + shifted(viscosity, offset_of(direction, 1)))
    lower_face = 0.5 * (middle + shifted(viscosity, offset_of(direction, -1)))
    return upper_face * (shifted(values, offset_of(direction, 1)) - center) - lower_face * (center - shifted(values, offset_of(direction, -1)))


def advance(padded):
    viscosity = base_viscosity + padded[4] / (padded[5] + wall_rate)
    centers = [shifted(padded[component], (0, 0, 0)) for component in range(6)]
    strain = jnp.zeros_like(centers[0])
    updated = []
    for component in range(3):
        change = -derivative(padded[3], component)
        for direction in range(3):
            gradient = derivative(padded[component], direction)
            strain = strain + gradient * gradient
            change = change - centers[direction] * gradient + diffusion(padded[component], viscosity, direction)
        updated.append(centers[component] + time_step * change)
    eddy_viscosity = centers[4] / (centers[5] + wall_rate)
    energy_change = eddy_viscosity * strain - beta_star * centers[4] * centers[5]
    rate_change = alpha_rate * strain - beta_rate * centers[5] * centers[5]
    for direction in range(3):
        energy_change = energy_change - centers[direction] * derivative(padded[4], direction) + diffusion(padded[4], viscosity, direction)
        rate_change = rate_change - centers[direction] * derivative(padded[5], direction) + diffusion(padded[5], viscosity, direction)
    return jnp.stack(updated), centers[4] + time_step * energy_change, centers[5] + time_step * rate_change


def side_weight(fraction, upper_side):
    if upper_side:
        return fraction
    return 1.0 - fraction


def reference(velocity, pressure, kinetic_energy, dissipation_rate, corner_ids, fractions, sector_owner):
    stacked = jnp.concatenate([velocity, pressure[None], kinetic_energy[None], dissipation_rate[None]], axis=0)
    padded = jnp.pad(stacked, ((0, 0), (2, 2), (2, 2), (2, 2)))
    new_velocity, new_energy, new_rate = advance(padded)
    flat_field = new_velocity.reshape(3, -1)
    plane_cells = CG * NR
    stream_cell = corner_ids // plane_cells
    remainder = corner_ids - stream_cell * plane_cells
    girth_cell = remainder // NR
    radial_cell = remainder - girth_cell * NR
    owners = jnp.repeat(sector_owner[:, 0], SW)
    girth_global = owners[None, :] * CG + girth_cell
    sampled = jnp.zeros((3, NRAD, NAZ), jnp.float32)
    for along_s in (0, 1):
        for along_g in (0, 1):
            for along_r in (0, 1):
                weight = side_weight(fractions[0], along_s) * side_weight(fractions[1], along_g) * side_weight(fractions[2], along_r)
                position = ((stream_cell + along_s) * NG + girth_global + along_g) * NR + radial_cell + along_r
                picked = jnp.take(flat_field, position.reshape(-1).astype(jnp.int32), axis=1).reshape(3, NRAD, NAZ)
                sampled = sampled + weight * picked
    spectrum = jnp.fft.rfft(sampled, axis=2, norm="ortho")[:, :, :NH]
    pieces = jnp.stack([jnp.real(spectrum), jnp.imag(spectrum)], axis=1).astype(jnp.float32)
    harmonics = jnp.transpose(pieces, (2, 0, 1, 3)).reshape(NRAD, 6 * NH)
    return new_velocity, new_energy, new_rate, harmonics
```

```python
import functools
import math

import jax
import jax.numpy as jnp
import numpy as np
from jax import lax
from jax.experimental import pallas as pl
from jax.experimental.pallas import tpu as pltpu
from jax.sharding import PartitionSpec as P

F32 = jnp.float32
BF16 = jnp.bfloat16
MESH = pl.DeviceIdType.MESH

base_viscosity = 0.05
time_step = 0.2
beta_star = 0.09
beta_rate = 0.075
alpha_rate = 0.52
wall_rate = 1.0

STREAM = 8
GIRTH = 16
RING = 4
PLANE = 32
CELLS_S = 4
CELLS_G = 8
CELLS_R = 256
AZIMUTHS = 1024
MODES = 128
SECTORS = 64
WIDTH = 16
ROWS = 3 * CELLS_S * CELLS_G
TILES = 24


def fourier_parts():
    a = np.arange(AZIMUTHS)[:, None]
    h = np.arange(MODES)[None, :]
    angle = (a * h % AZIMUTHS) * (2.0 * math.pi / AZIMUTHS)
    table = np.concatenate([np.cos(angle), -np.sin(angle)], axis=1) / math.sqrt(AZIMUTHS)
    table = table.astype(np.float32)
    high = table.astype(jnp.bfloat16)
    low = (table - high.astype(np.float32)).astype(jnp.bfloat16)
    return np.concatenate([high, low], axis=1)


def parts_of(x, count):
    parts = []
    for _ in range(count):
        part = x.astype(BF16)
        parts.append(part)
        x = x - part.astype(F32)
    return parts


def slope(up1, down1, up2, down2):
    return (8.0 * (up1 - down1) - (up2 - down2)) * (1.0 / 12.0)


def viscosity_of(energy, rate):
    return base_viscosity + energy / (rate + wall_rate)


def lane_shift(x, amount, fill):
    lane = lax.broadcasted_iota(jnp.int32, x.shape, 1)
    rolled = pltpu.roll(x, (-amount) % CELLS_R, axis=1)
    inside = (lane + amount >= 0) & (lane + amount < CELLS_R)
    return jnp.where(inside, rolled, fill)


def flux(center, up, down, v, v_up, v_down):
    return 0.5 * (v + v_up) * (up - center) - 0.5 * (v + v_down) * (center - down)


def stencil_layer(cells, above, wide, s):
    def at(f, ds, dg):
        if dg != 0:
            return wide[f, s, 8 + dg : 16 + dg, :]
        if s + ds < 0:
            return above[0, f, 2 + s + ds]
        if s + ds >= CELLS_S:
            return above[1, f, s + ds - CELLS_S]
        return cells[f, s + ds]

    v = viscosity_of(at(4, 0, 0), at(5, 0, 0))
    v_side = [
        [viscosity_of(at(4, d, 0), at(5, d, 0)) for d in (1, -1)],
        [viscosity_of(at(4, 0, d), at(5, 0, d)) for d in (1, -1)],
        [lane_shift(v, d, base_viscosity) for d in (1, -1)],
    ]
    centers = [at(f, 0, 0) for f in range(6)]

    def around(f, d):
        if d == 0:
            return [at(f, j, 0) for j in (1, -1, 2, -2)]
        if d == 1:
            return [at(f, 0, j) for j in (1, -1, 2, -2)]
        return [lane_shift(centers[f], j, 0.0) for j in (1, -1, 2, -2)]

    strain = None
    updated = []
    for c in range(3):
        change = -slope(*around(3, c))
        for d in range(3):
            near = around(c, d)
            gradient = slope(*near)
            square = gradient * gradient
            strain = square if strain is None else strain + square
            change = change - centers[d] * gradient
            change = change + flux(centers[c], near[0], near[1], v, *v_side[d])
        updated.append(centers[c] + time_step * change)
    eddy = centers[4] / (centers[5] + wall_rate)
    changes = [
        eddy * strain - beta_star * centers[4] * centers[5],
        alpha_rate * strain - beta_rate * centers[5] * centers[5],
    ]
    for i, f in enumerate((4, 5)):
        change = changes[i]
        for d in range(3):
            near = around(f, d)
            change = change - centers[d] * slope(*near)
            change = change + flux(centers[f], near[0], near[1], v, *v_side[d])
        updated.append(centers[f] + time_step * change)
    return updated


def point_tiles(a):
    lane = lax.broadcasted_iota(jnp.int32, (16, 128), 1)
    first = jnp.concatenate([a[0:16, 0:128], a[16:32, 0:128]], axis=1)
    rest = jnp.where(lane < 64, a[0:16, 128:256], a[16:32, 128:256])
    rest = jnp.concatenate([rest[0:8], rest[8:16]], axis=1)
    return jnp.concatenate([first, rest], axis=0)


def radius_rows(d):
    lane = lax.broadcasted_iota(jnp.int32, (16, 128), 1)
    first = jnp.concatenate([d[0:16, 0:128], d[0:16, 128:256]], axis=0)
    rest = jnp.concatenate([d[16:24, 0:128], d[16:24, 128:256]], axis=0)
    low = jnp.where(lane < 64, rest, 0.0)
    high = jnp.where(lane < 64, 0.0, rest)
    return jnp.concatenate([first, jnp.concatenate([low, high], axis=0)], axis=1)


def kernel(
    vel, pre, kin, dis, ids, frac, owner, ftab,
    nv_o, ne_o, nr_o, harm_o,
    cells, above, wide, pack, edge, nv, ids_v, frac_v, ft, choose, W, lhs, vec, acc, disk, four, sendb, recvb,
    in_sem, hs_sem, hr_sem, gs_sem, gr_sem, as_sem, ar_sem,
):
    t = lax.axis_index("stream")
    g = lax.axis_index("girth")
    y = t // RING
    z = lax.rem(t, RING)
    me = y * GIRTH + g

    own = [
        pltpu.make_async_copy(vel, cells.at[0:3], in_sem.at[0]),
        pltpu.make_async_copy(pre, cells.at[3], in_sem.at[1]),
        pltpu.make_async_copy(kin, cells.at[4], in_sem.at[2]),
        pltpu.make_async_copy(dis, cells.at[5], in_sem.at[3]),
    ]
    points = []
    for half in range(2):
        rows = pl.ds((half * RING + z) * GIRTH, GIRTH)
        points.append(
            pltpu.make_async_copy(ids.at[rows, :], ids_v.at[half], in_sem.at[4 + half])
        )
        points.append(
            pltpu.make_async_copy(frac.at[:, rows, :], frac_v.at[half], in_sem.at[6 + half])
        )
    points.append(pltpu.make_async_copy(ftab, ft, in_sem.at[8]))
    for copy in own + points:
        copy.start()

    barrier = pltpu.get_barrier_semaphore()

    def plane_peer(i):
        other = lax.rem(me + i, PLANE)
        return other, (other // GIRTH * RING + z, lax.rem(other, GIRTH))

    def ring_peer(i):
        return (y * RING + lax.rem(z + i, RING), g)

    def greet(i, carry):
        pl.semaphore_signal(barrier, inc=1, device_id=plane_peer(i)[1], device_id_type=MESH)
        return carry

    for i in range(1, RING):
        pl.semaphore_signal(barrier, inc=1, device_id=ring_peer(i), device_id_type=MESH)
    seam_up = t == RING - 1
    seam_down = t == RING

    @pl.when(seam_up)
    def _():
        pl.semaphore_signal(barrier, inc=1, device_id=(t + 1, g), device_id_type=MESH)

    @pl.when(seam_down)
    def _():
        pl.semaphore_signal(barrier, inc=1, device_id=(t - 1, g), device_id_type=MESH)

    lax.fori_loop(1, PLANE, greet, 0)

    for copy in own:
        copy.wait()
    for f in range(6):
        for s in range(CELLS_S):
            pack[0, f, 2 * s : 2 * s + 2, :] = cells[f, s, 0:2, :]
            pack[1, f, 2 * s : 2 * s + 2, :] = cells[f, s, 6:8, :]
            wide[f, s, 8:16, :] = cells[f, s]

    seam = jnp.where(seam_up | seam_down, 1, 0)
    pl.semaphore_wait(barrier, PLANE - 1 + RING - 1 + seam)

    def halo(k):
        if k == 0:
            src, dst, dev = cells.at[:, 0:2], above.at[1], (t - 1, g)
        elif k == 1:
            src, dst, dev = cells.at[:, 2:4], above.at[0], (t + 1, g)
        elif k == 2:
            src, dst, dev = pack.at[0], edge.at[1], (t, g - 1)
        else:
            src, dst, dev = pack.at[1], edge.at[0], (t, g + 1)
        return pltpu.make_async_remote_copy(
            src_ref=src, dst_ref=dst, send_sem=hs_sem.at[k], recv_sem=hr_sem.at[k],
            device_id=dev, device_id_type=MESH,
        )

    sends = (t > 0, t < STREAM - 1, g > 0, g < GIRTH - 1)
    receives = (sends[1], sends[0], sends[3], sends[2])
    for k in range(4):
        pl.when(sends[k])(lambda k=k: halo(k).start())

    @pl.when(t == 0)
    def _():
        above[0] = jnp.zeros((6, 2, 8, CELLS_R), F32)

    @pl.when(t == STREAM - 1)
    def _():
        above[1] = jnp.zeros((6, 2, 8, CELLS_R), F32)

    @pl.when(g == 0)
    def _():
        edge[0] = jnp.zeros((6, 8, CELLS_R), F32)

    @pl.when(g == GIRTH - 1)
    def _():
        edge[1] = jnp.zeros((6, 8, CELLS_R), F32)

    sub8 = lax.broadcasted_iota(jnp.int32, (8, 128), 0)
    lane8 = lax.broadcasted_iota(jnp.int32, (8, 128), 1)

    def sector(s, carry):
        count, place = carry
        mine = jnp.where(owner[s, 0] == g, 1, 0)
        here = (sub8 == s // 8) & (lane8 // WIDTH == lax.rem(s, 8))
        value = jnp.where(mine > 0, count * WIDTH, -AZIMUTHS) + lax.rem(lane8, WIDTH)
        return count + mine, jnp.where(here, value, place)

    _, place = lax.fori_loop(
        0, SECTORS, sector, (jnp.int32(0), jnp.full((8, 128), -AZIMUTHS, jnp.int32))
    )
    row = lax.broadcasted_iota(jnp.int32, (256, 128), 0)
    slot = jnp.where(row < 192, row, row - 64)
    for k in range(8):
        hit = slot == place[k : k + 1, :]
        choose[:, k * 128 : (k + 1) * 128] = jnp.where(hit, 1.0, 0.0).astype(BF16)

    for copy in points:
        copy.wait()
    cid = ids_v[...].reshape(PLANE, AZIMUTHS)
    stream_cell = lax.shift_right_logical(cid, 11)
    girth_cell = lax.shift_right_logical(cid, 8) & 7
    wall_cell = cid & 255
    stack = [wall_cell.astype(F32).astype(BF16), stream_cell.astype(F32).astype(BF16)]
    stack.append(girth_cell.astype(F32).astype(BF16))
    for i in range(3):
        stack.extend(parts_of(frac_v[:, i].reshape(PLANE, AZIMUTHS), 3))
    picked = lax.dot_general(
        jnp.concatenate(stack, axis=0), choose[...], (((1,), (1,)), ((), ())),
        preferred_element_type=F32,
    )
    part = [picked[32 * i : 32 * i + 32] for i in range(12)]
    cell_q, cell_s, cell_g = [point_tiles(part[i]) for i in range(3)]
    f_s, f_g, f_q = [
        point_tiles(part[3 + 3 * i] + part[4 + 3 * i] + part[5 + 3 * i]) for i in range(3)
    ]
    vec[0] = cell_s
    vec[1] = f_s
    vec[2] = cell_g
    vec[3] = f_g
    vec[4] = cell_q
    low_parts = parts_of(1.0 - f_q, 2)
    high_parts = parts_of(f_q, 2)
    vec[5] = low_parts[0].astype(F32)
    vec[6] = low_parts[1].astype(F32)
    vec[7] = high_parts[0].astype(F32)
    vec[8] = high_parts[1].astype(F32)

    chosen = jnp.dot(choose[...], ft[...], preferred_element_type=F32).astype(BF16)
    four[0:256, :] = chosen[:, 0:256]
    four[256:512, :] = chosen[:, 0:256]
    four[512:768, :] = chosen[:, 256:512]

    def weights(n, carry):
        def v(i):
            return vec[i, pl.ds(n, 1), :]

        q = lax.broadcasted_iota(jnp.int32, (CELLS_R, 256), 0).astype(F32)
        at_q = q == v(4)
        at_up = q == v(4) + 1.0
        high = jnp.where(at_q, v(5), jnp.where(at_up, v(7), 0.0)).astype(BF16)
        low = jnp.where(at_q, v(6), jnp.where(at_up, v(8), 0.0)).astype(BF16)
        cols = pl.ds(pl.multiple_of(n * 256, 256), 256)
        W[0:256, cols] = high
        W[256:512, cols] = high
        W[512:768, cols] = low
        return carry

    lax.fori_loop(0, TILES, weights, 0)
    sendb[...] = jnp.zeros_like(sendb)

    for k in range(4):
        pl.when(receives[k])(lambda k=k: halo(k).wait_recv())
    for f in range(6):
        for s in range(CELLS_S):
            wide[f, s, 6:8, :] = edge[0, f, 2 * s : 2 * s + 2, :]
            wide[f, s, 16:18, :] = edge[1, f, 2 * s : 2 * s + 2, :]
    for s in range(CELLS_S):
        updated = stencil_layer(cells, above, wide, s)
        for c in range(3):
            nv[0, c * 32 + s * 8 : c * 32 + s * 8 + 8, :] = updated[c]
        ne_o[s] = updated[3]
        nr_o[s] = updated[4]

    def gather(i):
        return pltpu.make_async_remote_copy(
            src_ref=nv.at[0], dst_ref=nv.at[RING - i], send_sem=gs_sem.at[i], recv_sem=gr_sem.at[i],
            device_id=ring_peer(i), device_id_type=MESH,
        )

    def gathered(i):
        return gather(RING - i)

    for i in (1, 3, 2):
        gather(i).start()
    for c in range(3):
        for s in range(CELLS_S):
            nv_o[c, s] = nv[0, c * 32 + s * 8 : c * 32 + s * 8 + 8, :]

    def load_block(i):
        high, low = parts_of(nv[i], 2)
        lhs[i * ROWS : (i + 1) * ROWS, :] = jnp.concatenate([high, low, high], axis=1)

    def layers(blocks, n, sums):
        first, count = blocks
        cols = pl.ds(pl.multiple_of(n * 256, 256), 256)
        out = jnp.dot(
            lhs[first * ROWS : (first + count) * ROWS, :], W[:, cols],
            preferred_element_type=F32,
        )
        cell = jnp.broadcast_to(vec[0, pl.ds(n, 1), :], (8, 256))
        up = jnp.broadcast_to(vec[1, pl.ds(n, 1), :], (8, 256))
        stay = 1.0 - up
        for b in range(count):
            base = ((y * RING + lax.rem(z + first + b, RING)) * CELLS_S).astype(F32)
            above = cell - base
            for s in range(CELLS_S):
                weight = jnp.where(above == s, stay, jnp.where(above == s - 1, up, 0.0))
                for c in range(3):
                    at = b * ROWS + c * 32 + s * 8
                    term = weight * out[at : at + 8]
                    sums[c] = term if sums[c] is None else sums[c] + term
        return sums

    load_block(0)

    def first_pass(n, carry):
        sums = layers((0, 1), n, [None] * 3)
        for c in range(3):
            acc[c * TILES + n] = sums[c]
        return carry

    lax.fori_loop(0, TILES, first_pass, 0)

    for i in (1, 3, 2):
        gathered(i).wait_recv()
        load_block(i)

    def second_pass(n, carry):
        sums = layers((1, 3), n, [acc[c * TILES + n] for c in range(3)])
        cell = vec[2, pl.ds(n, 1), :]
        up = vec[3, pl.ds(n, 1), :]
        side = lax.broadcasted_iota(jnp.int32, (8, 256), 0).astype(F32)
        weight = jnp.where(side == cell, 1.0 - up, jnp.where(side == cell + 1.0, up, 0.0))
        for c in range(3):
            disk[pl.ds(c * TILES + n, 1), :] = jnp.sum(sums[c] * weight, axis=0, keepdims=True)
        return carry

    lax.fori_loop(0, TILES, second_pass, 0)

    rows = jnp.concatenate(
        [radius_rows(disk[c * TILES : (c + 1) * TILES, :]) for c in range(3)], axis=0
    )
    high, low = parts_of(rows, 2)
    spectrum = jnp.dot(
        jnp.concatenate([high, low, high], axis=1), four[...], preferred_element_type=F32
    )
    for c in range(3):
        for k in range(2):
            sendb[pl.ds(2 * c + k, PLANE, stride=8), :] = spectrum[
                c * PLANE : (c + 1) * PLANE, k * 128 : (k + 1) * 128
            ]

    def slot_of(i):
        return pl.ds(pl.multiple_of(i * 8, 8), 8)

    def post(i):
        other, dev = plane_peer(i)
        return pltpu.make_async_remote_copy(
            src_ref=sendb.at[slot_of(other), :], dst_ref=recvb.at[slot_of(i), :],
            send_sem=as_sem.at[i], recv_sem=ar_sem.at[i], device_id=dev, device_id_type=MESH,
        )

    def post_one(i, carry):
        post(i).start()
        return carry

    lax.fori_loop(1, PLANE, post_one, 0)

    def take_one(i, carry):
        post(i).wait_recv()
        return carry

    lax.fori_loop(1, PLANE, take_one, 0)
    total = sendb[slot_of(me), :]
    for i in range(1, PLANE):
        total = total + recvb[8 * i : 8 * i + 8, :]
    for k in range(6):
        harm_o[0:1, k * 128 : (k + 1) * 128] = total[k : k + 1, :]

    for k in range(4):
        pl.when(sends[k])(lambda k=k: halo(k).wait_send())
    for i in range(1, RING):
        gather(i).wait_send()

    def sent_one(i, carry):
        post(i).wait_send()
        return carry

    lax.fori_loop(1, PLANE, sent_one, 0)


def body(velocity, pressure, kinetic_energy, dissipation_rate, corner_ids, fractions, sector_owner):
    hbm = pl.BlockSpec(memory_space=pltpu.HBM)
    vmem = pl.BlockSpec(memory_space=pltpu.VMEM)
    smem = pl.BlockSpec(memory_space=pltpu.SMEM)
    dma = pltpu.SemaphoreType.DMA
    return pl.pallas_call(
        kernel,
        out_shape=(
            jax.ShapeDtypeStruct(velocity.shape, F32),
            jax.ShapeDtypeStruct(pressure.shape, F32),
            jax.ShapeDtypeStruct(pressure.shape, F32),
            jax.ShapeDtypeStruct((1, 6 * MODES), F32),
        ),
        in_specs=[hbm] * 6 + [smem, hbm],
        out_specs=(vmem,) * 4,
        scratch_shapes=[
            pltpu.VMEM((6, CELLS_S, CELLS_G, CELLS_R), F32),
            pltpu.VMEM((2, 6, 2, CELLS_G, CELLS_R), F32),
            pltpu.VMEM((6, CELLS_S, 24, CELLS_R), F32),
            pltpu.VMEM((2, 6, 8, CELLS_R), F32),
            pltpu.VMEM((2, 6, 8, CELLS_R), F32),
            pltpu.VMEM((RING, ROWS, CELLS_R), F32),
            pltpu.VMEM((2, GIRTH, AZIMUTHS), jnp.int32),
            pltpu.VMEM((2, 3, GIRTH, AZIMUTHS), F32),
            pltpu.VMEM((AZIMUTHS, 512), BF16),
            pltpu.VMEM((256, AZIMUTHS), BF16),
            pltpu.VMEM((768, TILES * 256), BF16),
            pltpu.VMEM((RING * ROWS, 768), BF16),
            pltpu.VMEM((9, TILES, 256), F32),
            pltpu.VMEM((3 * TILES, 8, 256), F32),
            pltpu.VMEM((3 * TILES, 256), F32),
            pltpu.VMEM((768, 256), BF16),
            pltpu.VMEM((PLANE * 8, 128), F32),
            pltpu.VMEM((PLANE * 8, 128), F32),
            dma((9,)),
            dma((4,)),
            dma((4,)),
            dma((RING,)),
            dma((RING,)),
            dma((PLANE,)),
            dma((PLANE,)),
        ],
        compiler_params=pltpu.CompilerParams(
            collective_id=0, has_side_effects=True, vmem_limit_bytes=48 * 1024 * 1024
        ),
    )(
        velocity, pressure, kinetic_energy, dissipation_rate, corner_ids, fractions, sector_owner,
        jnp.asarray(fourier_parts()),
    )


def solution(mesh):
    return jax.shard_map(
        body,
        mesh=mesh,
        in_specs=(
            P(None, "stream", "girth", None),
            P("stream", "girth", None),
            P("stream", "girth", None),
            P("stream", "girth", None),
            P(),
            P(),
            P(),
        ),
        out_specs=(
            P(None, "stream", "girth", None),
            P("stream", "girth", None),
            P("stream", "girth", None),
            P(("stream", "girth"), None),
        ),
        check_vma=False,
    )
```

```python
import functools
import math

import jax
import jax.numpy as jnp
import numpy as np
from jax import lax
from jax.experimental import pallas as pl
from jax.experimental.pallas import tpu as pltpu
from jax.sharding import PartitionSpec as P

F32 = jnp.float32
BF16 = jnp.bfloat16
MESH = pl.DeviceIdType.MESH

base_viscosity = 0.05
time_step = 0.2
beta_star = 0.09
beta_rate = 0.075
alpha_rate = 0.52
wall_rate = 1.0

STREAM = 8
GIRTH = 16
RING = 4
PLANE = 32
CELLS_S = 4
CELLS_G = 8
CELLS_R = 256
AZIMUTHS = 1024
MODES = 128
SECTORS = 64
WIDTH = 16
ROWS = 3 * CELLS_S * CELLS_G
TILES = 24
HALF = TILES // 2
VMEM_BYTES = 64 * 1024 * 1024


def fourier_parts():
    a = np.arange(AZIMUTHS)[:, None]
    h = np.arange(MODES)[None, :]
    angle = (a * h % AZIMUTHS) * (2.0 * math.pi / AZIMUTHS)
    table = np.concatenate([np.cos(angle), -np.sin(angle)], axis=1) / math.sqrt(AZIMUTHS)
    table = table.astype(np.float32)
    high = table.astype(jnp.bfloat16)
    low = (table - high.astype(np.float32)).astype(jnp.bfloat16)
    return np.concatenate([high, low], axis=1)


def parts_of(x, count):
    parts = []
    for _ in range(count):
        part = x.astype(BF16)
        parts.append(part)
        x = x - part.astype(F32)
    return parts


def slope(up1, down1, up2, down2):
    return (8.0 * (up1 - down1) - (up2 - down2)) * (1.0 / 12.0)


def viscosity_of(energy, rate):
    return base_viscosity + energy / (rate + wall_rate)


def lane_shift(x, amount, fill):
    lane = lax.broadcasted_iota(jnp.int32, x.shape, 1)
    rolled = pltpu.roll(x, (-amount) % CELLS_R, axis=1)
    inside = (lane + amount >= 0) & (lane + amount < CELLS_R)
    return jnp.where(inside, rolled, fill)


def flux(center, up, down, v, v_up, v_down):
    return 0.5 * (v + v_up) * (up - center) - 0.5 * (v + v_down) * (center - down)


class Layer:
    def __init__(self, cells, above, wide, s):
        self.cells, self.above, self.wide, self.s = cells, above, wide, s
        self.v = viscosity_of(self.at(4, 0, 0), self.at(5, 0, 0))
        self.v_side = [
            [viscosity_of(self.at(4, d, 0), self.at(5, d, 0)) for d in (1, -1)],
            [viscosity_of(self.at(4, 0, d), self.at(5, 0, d)) for d in (1, -1)],
            [lane_shift(self.v, d, base_viscosity) for d in (1, -1)],
        ]
        self.centers = [self.at(f, 0, 0) for f in range(6)]

    def at(self, f, ds, dg):
        s = self.s
        if dg != 0:
            return self.wide[f, s, 8 + dg : 16 + dg, :]
        if s + ds < 0:
            return self.above[0, f, 2 + s + ds]
        if s + ds >= CELLS_S:
            return self.above[1, f, s + ds - CELLS_S]
        return self.cells[f, s + ds]

    def around(self, f, d):
        if d == 0:
            return [self.at(f, j, 0) for j in (1, -1, 2, -2)]
        if d == 1:
            return [self.at(f, 0, j) for j in (1, -1, 2, -2)]
        return [lane_shift(self.centers[f], j, 0.0) for j in (1, -1, 2, -2)]

    def diffuse(self, f, near, d):
        return flux(self.centers[f], near[0], near[1], self.v, *self.v_side[d])

    def velocity(self):
        strain = None
        updated = []
        for c in range(3):
            change = -slope(*self.around(3, c))
            for d in range(3):
                near = self.around(c, d)
                gradient = slope(*near)
                square = gradient * gradient
                strain = square if strain is None else strain + square
                change = change - self.centers[d] * gradient
                change = change + self.diffuse(c, near, d)
            updated.append(self.centers[c] + time_step * change)
        return updated, strain

    def turbulence(self, strain):
        k, w = self.centers[4], self.centers[5]
        changes = [
            k / (w + wall_rate) * strain - beta_star * k * w,
            alpha_rate * strain - beta_rate * w * w,
        ]
        updated = []
        for change, f in zip(changes, (4, 5)):
            for d in range(3):
                near = self.around(f, d)
                change = change - self.centers[d] * slope(*near)
                change = change + self.diffuse(f, near, d)
            updated.append(self.centers[f] + time_step * change)
        return updated


def point_tiles(a):
    lane = lax.broadcasted_iota(jnp.int32, (16, 128), 1)
    first = jnp.concatenate([a[0:16, 0:128], a[16:32, 0:128]], axis=1)
    rest = jnp.where(lane < 64, a[0:16, 128:256], a[16:32, 128:256])
    tiles = []
    for h in range(2):
        tiles.append(first[8 * h : 8 * h + 8])
        both = [rest[8 * h : 8 * h + 4], rest[8 * h + 4 : 8 * h + 8]]
        tiles.append(jnp.concatenate(both, axis=1))
    return jnp.concatenate(tiles, axis=0)


def radius_rows(d):
    lane = lax.broadcasted_iota(jnp.int32, (8, 128), 1)
    rest = jnp.concatenate([d[8:12, 0:128], d[8:12, 128:256]], axis=0)
    low = jnp.where(lane < 64, rest, 0.0)
    high = jnp.where(lane < 64, 0.0, rest)
    return jnp.concatenate(
        [
            jnp.concatenate([d[0:8, 0:128], low], axis=1),
            jnp.concatenate([d[0:8, 128:256], high], axis=1),
        ],
        axis=0,
    )


def kernel(
    vel, pre, kin, dis, ids, frac, owner, ftab,
    nv_o, ne_o, nr_o, harm_o,
    cells, above, wide, pack, edge, nv, strain_v, turb, ids_v, frac_v, ft, choose, W, lhs, vec,
    acc, disk, four, sendb, recvb,
    in_sem, out_sem, hs_sem, hr_sem, gs_sem, gr_sem, as_sem, ar_sem,
):
    t = lax.axis_index("stream")
    g = lax.axis_index("girth")
    y = t // RING
    z = lax.rem(t, RING)
    me = y * GIRTH + g

    own = [
        pltpu.make_async_copy(vel, cells.at[0:3], in_sem.at[0]),
        pltpu.make_async_copy(pre, cells.at[3], in_sem.at[1]),
        pltpu.make_async_copy(kin, cells.at[4], in_sem.at[2]),
        pltpu.make_async_copy(dis, cells.at[5], in_sem.at[3]),
    ]
    for copy in own:
        copy.start()

    barrier = pltpu.get_barrier_semaphore()

    def plane_peer(i):
        other = lax.rem(me + i, PLANE)
        return other, (other // GIRTH * RING + z, lax.rem(other, GIRTH))

    def ring_peer(i):
        return (y * RING + lax.rem(z + i, RING), g)

    def greet(i, carry):
        pl.semaphore_signal(barrier, inc=1, device_id=plane_peer(i)[1], device_id_type=MESH)
        return carry

    seam_up = t == RING - 1
    seam_down = t == RING

    @pl.when(seam_up)
    def _():
        pl.semaphore_signal(barrier, inc=1, device_id=(t + 1, g), device_id_type=MESH)

    @pl.when(seam_down)
    def _():
        pl.semaphore_signal(barrier, inc=1, device_id=(t - 1, g), device_id_type=MESH)

    for i in (1, RING - 1, 2):
        pl.semaphore_signal(barrier, inc=1, device_id=ring_peer(i), device_id_type=MESH)
    greet(1, 0)
    greet(PLANE - 1, 0)
    lax.fori_loop(2, PLANE - 1, greet, 0)

    points = []
    for half in range(2):
        rows = pl.ds((half * RING + z) * GIRTH, GIRTH)
        points.append(
            pltpu.make_async_copy(ids.at[rows, :], ids_v.at[half], in_sem.at[4 + half])
        )
        points.append(
            pltpu.make_async_copy(frac.at[:, rows, :], frac_v.at[half], in_sem.at[6 + half])
        )
    points.append(pltpu.make_async_copy(ftab, ft, in_sem.at[8]))

    seam = jnp.where(seam_up | seam_down, 1, 0)
    pl.semaphore_wait(barrier, PLANE - 1 + RING - 1 + seam)

    def halo(k):
        if k < 8:
            down = k < 4
            field, place = ((vel, pl.ds(0, 3)), (pre, 3), (kin, 4), (dis, 5))[k % 4]
            layers_of = pl.ds(0, 2) if down else pl.ds(2, 2)
            src = field.at[:, layers_of] if k % 4 == 0 else field.at[layers_of]
            dst = above.at[1 if down else 0, place]
            dev = (t - 1, g) if down else (t + 1, g)
        elif k == 8:
            src, dst, dev = pack.at[0], edge.at[1], (t, g - 1)
        else:
            src, dst, dev = pack.at[1], edge.at[0], (t, g + 1)
        return pltpu.make_async_remote_copy(
            src_ref=src, dst_ref=dst, send_sem=hs_sem.at[k], recv_sem=hr_sem.at[k],
            device_id=dev, device_id_type=MESH,
        )

    sides = (range(0, 4), range(4, 8), range(8, 9), range(9, 10))
    sends = (t > 0, t < STREAM - 1, g > 0, g < GIRTH - 1)
    receives = (sends[1], sends[0], sends[3], sends[2])

    def each(side, there, act):
        @pl.when(there[side])
        def _():
            for k in sides[side]:
                act(halo(k))

    for side in (0, 1):
        each(side, sends, lambda copy: copy.start())
    for copy in own:
        copy.wait()
    for f in range(6):
        for s in range(CELLS_S):
            pack[0, f, 2 * s : 2 * s + 2, :] = cells[f, s, 0:2, :]
            pack[1, f, 2 * s : 2 * s + 2, :] = cells[f, s, 6:8, :]
    for side in (2, 3):
        each(side, sends, lambda copy: copy.start())
    for copy in points:
        copy.start()
    for f in range(6):
        for s in range(CELLS_S):
            wide[f, s, 8:16, :] = cells[f, s]

    @pl.when(t == 0)
    def _():
        above[0] = jnp.zeros((6, 2, 8, CELLS_R), F32)

    @pl.when(t == STREAM - 1)
    def _():
        above[1] = jnp.zeros((6, 2, 8, CELLS_R), F32)

    @pl.when(g == 0)
    def _():
        edge[0] = jnp.zeros((6, 8, CELLS_R), F32)

    @pl.when(g == GIRTH - 1)
    def _():
        edge[1] = jnp.zeros((6, 8, CELLS_R), F32)

    sub8 = lax.broadcasted_iota(jnp.int32, (8, 128), 0)
    lane8 = lax.broadcasted_iota(jnp.int32, (8, 128), 1)

    def sector(s, carry):
        count, place = carry
        mine = jnp.where(owner[s] == g, 1, 0)
        here = (sub8 == s // 8) & (lane8 // WIDTH == lax.rem(s, 8))
        value = jnp.where(mine > 0, count * WIDTH, -AZIMUTHS) + lax.rem(lane8, WIDTH)
        return count + mine, jnp.where(here, value, place)

    _, place = lax.fori_loop(
        0, SECTORS, sector, (jnp.int32(0), jnp.full((8, 128), -AZIMUTHS, jnp.int32))
    )
    row = lax.broadcasted_iota(jnp.int32, (256, 128), 0)
    slot = jnp.where(row < 192, row, row - 64)
    for k in range(8):
        hit = slot == place[k : k + 1, :]
        choose[:, k * 128 : (k + 1) * 128] = jnp.where(hit, 1.0, 0.0).astype(BF16)

    for copy in points:
        copy.wait()
    cid = ids_v[...].reshape(PLANE, AZIMUTHS)
    stream_cell = lax.shift_right_logical(cid, 11)
    girth_cell = lax.shift_right_logical(cid, 8) & 7
    wall_cell = cid & 255
    stack = [wall_cell.astype(F32).astype(BF16), stream_cell.astype(F32).astype(BF16)]
    stack.append(girth_cell.astype(F32).astype(BF16))
    for i in range(3):
        stack.extend(parts_of(frac_v[:, i].reshape(PLANE, AZIMUTHS), 3))
    picked = lax.dot_general(
        jnp.concatenate(stack, axis=0), choose[...], (((1,), (1,)), ((), ())),
        preferred_element_type=F32,
    )
    part = [picked[32 * i : 32 * i + 32] for i in range(12)]
    cell_q, cell_s, cell_g = [point_tiles(part[i]) for i in range(3)]
    f_s, f_g, f_q = [
        point_tiles(part[3 + 3 * i] + part[4 + 3 * i] + part[5 + 3 * i]) for i in range(3)
    ]
    vec[0] = cell_s
    vec[1] = f_s
    vec[2] = cell_g
    vec[3] = f_g
    vec[4] = cell_q
    low_parts = parts_of(1.0 - f_q, 2)
    high_parts = parts_of(f_q, 2)
    vec[5] = low_parts[0].astype(F32)
    vec[6] = low_parts[1].astype(F32)
    vec[7] = high_parts[0].astype(F32)
    vec[8] = high_parts[1].astype(F32)

    chosen = jnp.dot(choose[...], ft[...], preferred_element_type=F32).astype(BF16)
    four[0:256, :] = chosen[:, 0:256]
    four[256:512, :] = chosen[:, 256:512]

    def weights(n, carry):
        def v(i):
            return vec[i, pl.ds(n, 1), :]

        q = lax.broadcasted_iota(jnp.int32, (CELLS_R, 256), 0).astype(F32)
        at_q = q == v(4)
        at_up = q == v(4) + 1.0
        high = jnp.where(at_q, v(5), jnp.where(at_up, v(7), 0.0)).astype(BF16)
        low = jnp.where(at_q, v(6), jnp.where(at_up, v(8), 0.0)).astype(BF16)
        cols = pl.ds(pl.multiple_of(n * 256, 256), 256)
        W[0:256, cols] = high
        W[256:512, cols] = low
        return carry

    lax.fori_loop(0, TILES, weights, 0, unroll=2)
    sendb[...] = jnp.zeros_like(sendb)

    for side in range(4):
        each(side, receives, lambda copy: copy.wait_recv())
    for f in range(6):
        for s in range(CELLS_S):
            wide[f, s, 6:8, :] = edge[0, f, 2 * s : 2 * s + 2, :]
            wide[f, s, 16:18, :] = edge[1, f, 2 * s : 2 * s + 2, :]

    def gather(i, s):
        return pltpu.make_async_remote_copy(
            src_ref=nv.at[0, s], dst_ref=nv.at[RING - i, s],
            send_sem=gs_sem.at[i * CELLS_S + s], recv_sem=gr_sem.at[i * CELLS_S + s],
            device_id=ring_peer(i), device_id_type=MESH,
        )

    for s in range(CELLS_S):
        updated, strain = Layer(cells, above, wide, s).velocity()
        for c in range(3):
            nv[0, s, c] = updated[c]
        strain_v[s] = strain
        for i in (2, 1, 3):
            gather(i, s).start()
    for s in range(CELLS_S):
        turb[0, s], turb[1, s] = Layer(cells, above, wide, s).turbulence(strain_v[s])
    results = [
        pltpu.make_async_copy(nv.at[0, s], nv_o.at[:, s], out_sem.at[s]) for s in range(CELLS_S)
    ]
    results.append(pltpu.make_async_copy(turb.at[0], ne_o, out_sem.at[4]))
    results.append(pltpu.make_async_copy(turb.at[1], nr_o, out_sem.at[5]))
    for copy in results:
        copy.start()

    def load_blocks(first, count):
        value = jnp.concatenate(
            [nv[first + b].reshape(ROWS, CELLS_R) for b in range(count)], axis=0
        )
        high, low = parts_of(value, 2)
        start = 2 * first * ROWS
        lhs[start : start + count * ROWS, :] = high
        lhs[start + count * ROWS : start + 2 * count * ROWS, :] = low

    def layers(blocks, n, sums):
        first, count = blocks
        start, rows = 2 * first * ROWS, count * ROWS
        cols = pl.ds(pl.multiple_of(n * 256, 256), 256)
        both = jnp.dot(
            lhs[start : start + 2 * rows, :], W[0:256, cols], preferred_element_type=F32
        )
        fine = jnp.dot(lhs[start : start + rows, :], W[256:512, cols], preferred_element_type=F32)
        out = both[0:rows] + both[rows : 2 * rows] + fine
        cell = jnp.broadcast_to(vec[0, pl.ds(n, 1), :], (8, 256))
        up = jnp.broadcast_to(vec[1, pl.ds(n, 1), :], (8, 256))
        stay = 1.0 - up
        for b in range(count):
            base = ((y * RING + lax.rem(z + first + b, RING)) * CELLS_S).astype(F32)
            above_base = cell - base
            for s in range(CELLS_S):
                weight = jnp.where(
                    above_base == s, stay, jnp.where(above_base == s - 1, up, 0.0)
                )
                for c in range(3):
                    at = b * ROWS + s * 24 + c * 8
                    term = weight * out[at : at + 8]
                    sums[c] = term if sums[c] is None else sums[c] + term
        return sums

    load_blocks(0, 1)

    def first_pass(n, carry):
        sums = layers((0, 1), n, [None] * 3)
        for c in range(3):
            acc[c * TILES + n] = sums[c]
        return carry

    lax.fori_loop(0, TILES, first_pass, 0, unroll=4)

    for i in range(1, RING):
        for s in range(CELLS_S):
            gather(i, s).wait_recv()
    load_blocks(1, RING - 1)

    near = g // 8
    my_slot = y * 8 + lax.rem(g, 8)

    def slot_of(i):
        return pl.ds(pl.multiple_of(i * 8, 8), 8)

    def post(turn, j):
        half = 1 - near if turn == 0 else near
        slot = lax.rem(my_slot + j, 16)
        dev = (slot // 8 * RING + z, half * 8 + lax.rem(slot, 8))
        return pltpu.make_async_remote_copy(
            src_ref=sendb.at[slot_of(16 * turn + slot), :],
            dst_ref=recvb.at[slot_of(16 * turn + j), :],
            send_sem=as_sem.at[turn], recv_sem=ar_sem.at[turn],
            device_id=dev, device_id_type=MESH,
        )

    def posts(turn):
        span = pl.ds(128 * turn + 8 * turn, 128 - 8 * turn)
        return pltpu.make_async_remote_copy(
            src_ref=sendb.at[span, :], dst_ref=recvb.at[span, :],
            send_sem=as_sem.at[turn], recv_sem=ar_sem.at[turn],
            device_id=plane_peer(1)[1], device_id_type=MESH,
        )

    for turn in range(2):
        offset = ((1 - near) if turn == 0 else near) * HALF

        def second_pass(k, carry, offset=offset):
            n = offset + k
            sums = layers((1, 3), n, [acc[c * TILES + n] for c in range(3)])
            cell = vec[2, pl.ds(n, 1), :]
            up = vec[3, pl.ds(n, 1), :]
            side = lax.broadcasted_iota(jnp.int32, (8, 256), 0).astype(F32)
            weight = jnp.where(side == cell, 1.0 - up, jnp.where(side == cell + 1.0, up, 0.0))
            for c in range(3):
                disk[pl.ds(c * 16 + k, 1), :] = jnp.sum(sums[c] * weight, axis=0, keepdims=True)
            return carry

        lax.fori_loop(0, HALF, second_pass, 0, unroll=4)
        rows = jnp.concatenate(
            [radius_rows(disk[c * 16 : c * 16 + HALF, :]) for c in range(3)], axis=0
        )
        high, low = parts_of(rows, 2)
        both = jnp.dot(
            jnp.concatenate([high, low], axis=0), four[0:256, :], preferred_element_type=F32
        )
        fine = jnp.dot(high, four[256:512, :], preferred_element_type=F32)
        spectrum = both[0:48] + both[48:96] + fine
        for c in range(3):
            for k in range(2):
                sendb[pl.ds(128 * turn + 2 * c + k, 16, stride=8), :] = spectrum[
                    c * 16 : (c + 1) * 16, k * 128 : (k + 1) * 128
                ]

        def post_one(j, carry, turn=turn):
            post(turn, j).start()
            return carry

        lax.fori_loop(turn, 16, post_one, 0)

    total = sendb[slot_of(16 + my_slot), :]
    for turn in range(2):
        posts(turn).wait_recv()
        for j in range(turn, 16):
            row = 128 * turn + 8 * j
            total = total + recvb[row : row + 8, :]
    for k in range(6):
        harm_o[0:1, k * 128 : (k + 1) * 128] = total[k : k + 1, :]

    for side in range(4):
        each(side, sends, lambda copy: copy.wait_send())
    for i in range(1, RING):
        for s in range(CELLS_S):
            gather(i, s).wait_send()
    for copy in results:
        copy.wait()
    for turn in range(2):
        posts(turn).wait_send()


def place_results(*refs):
    count = len(refs) // 2
    for i in range(count):
        refs[count + i][...] = refs[i][...]


def body(velocity, pressure, kinetic_energy, dissipation_rate, corner_ids, fractions, sector_owner):
    hbm = pl.BlockSpec(memory_space=pltpu.HBM)
    vmem = pl.BlockSpec(memory_space=pltpu.VMEM)
    smem = pl.BlockSpec(memory_space=pltpu.SMEM)
    dma = pltpu.SemaphoreType.DMA
    shapes = (
        jax.ShapeDtypeStruct(velocity.shape, F32),
        jax.ShapeDtypeStruct(pressure.shape, F32),
        jax.ShapeDtypeStruct(pressure.shape, F32),
        jax.ShapeDtypeStruct((1, 6 * MODES), F32),
    )
    results = pl.pallas_call(
        kernel,
        out_shape=shapes,
        in_specs=[hbm] * 6 + [smem, hbm],
        out_specs=(hbm, hbm, hbm, vmem),
        scratch_shapes=[
            pltpu.VMEM((6, CELLS_S, CELLS_G, CELLS_R), F32),
            pltpu.VMEM((2, 6, 2, CELLS_G, CELLS_R), F32),
            pltpu.VMEM((6, CELLS_S, 24, CELLS_R), F32),
            pltpu.VMEM((2, 6, 8, CELLS_R), F32),
            pltpu.VMEM((2, 6, 8, CELLS_R), F32),
            pltpu.VMEM((RING, CELLS_S, 3, CELLS_G, CELLS_R), F32),
            pltpu.VMEM((CELLS_S, CELLS_G, CELLS_R), F32),
            pltpu.VMEM((2, CELLS_S, CELLS_G, CELLS_R), F32),
            pltpu.VMEM((2, GIRTH, AZIMUTHS), jnp.int32),
            pltpu.VMEM((2, 3, GIRTH, AZIMUTHS), F32),
            pltpu.VMEM((AZIMUTHS, 512), BF16),
            pltpu.VMEM((256, AZIMUTHS), BF16),
            pltpu.VMEM((512, TILES * 256), BF16),
            pltpu.VMEM((2 * RING * ROWS, 256), BF16),
            pltpu.VMEM((9, TILES, 256), F32),
            pltpu.VMEM((3 * TILES, 8, 256), F32),
            pltpu.VMEM((48, 256), F32),
            pltpu.VMEM((512, 256), BF16),
            pltpu.VMEM((PLANE * 8, 128), F32),
            pltpu.VMEM((PLANE * 8, 128), F32),
            dma((9,)),
            dma((6,)),
            dma((10,)),
            dma((10,)),
            dma((RING * CELLS_S,)),
            dma((RING * CELLS_S,)),
            dma((2,)),
            dma((2,)),
        ],
        compiler_params=pltpu.CompilerParams(
            collective_id=0, has_side_effects=True, vmem_limit_bytes=VMEM_BYTES
        ),
    )(
        velocity, pressure, kinetic_energy, dissipation_rate, corner_ids, fractions,
        sector_owner.reshape(SECTORS), jnp.asarray(fourier_parts()),
    )
    return pl.pallas_call(
        place_results,
        out_shape=shapes,
        in_specs=[vmem] * 4,
        out_specs=(vmem,) * 4,
        compiler_params=pltpu.CompilerParams(vmem_limit_bytes=VMEM_BYTES),
    )(*results)


def solution(mesh):
    return jax.shard_map(
        body,
        mesh=mesh,
        in_specs=(
            P(None, "stream", "girth", None),
            P("stream", "girth", None),
            P("stream", "girth", None),
            P("stream", "girth", None),
            P(),
            P(),
            P(),
        ),
        out_specs=(
            P(None, "stream", "girth", None),
            P("stream", "girth", None),
            P("stream", "girth", None),
            P(("stream", "girth"), None),
        ),
        check_vma=False,
    )
```

```python
import functools
import math

import jax
import jax.numpy as jnp
import numpy as np
from jax import lax
from jax.experimental import pallas as pl
from jax.experimental.pallas import tpu as pltpu
from jax.sharding import PartitionSpec as P

F32 = jnp.float32
BF16 = jnp.bfloat16
MESH = pl.DeviceIdType.MESH

base_viscosity = 0.05
time_step = 0.2
beta_star = 0.09
beta_rate = 0.075
alpha_rate = 0.52
wall_rate = 1.0

STREAM = 8
GIRTH = 16
RING = 4
PLANE = 32
CELLS_S = 4
CELLS_G = 8
CELLS_R = 256
AZIMUTHS = 1024
MODES = 128
SECTORS = 64
WIDTH = 16
ROWS = 3 * CELLS_S * CELLS_G
TILES = 24
HALF = TILES // 2
VMEM_BYTES = 64 * 1024 * 1024


def fourier_parts():
    a = np.arange(AZIMUTHS)[:, None]
    h = np.arange(MODES)[None, :]
    angle = (a * h % AZIMUTHS) * (2.0 * math.pi / AZIMUTHS)
    table = np.concatenate([np.cos(angle), -np.sin(angle)], axis=1) / math.sqrt(AZIMUTHS)
    table = table.astype(np.float32)
    high = table.astype(jnp.bfloat16)
    low = (table - high.astype(np.float32)).astype(jnp.bfloat16)
    return np.concatenate([high, low], axis=1)


def parts_of(x, count):
    parts = []
    for _ in range(count):
        part = x.astype(BF16)
        parts.append(part)
        x = x - part.astype(F32)
    return parts


def slope(up1, down1, up2, down2):
    return (8.0 * (up1 - down1) - (up2 - down2)) * (1.0 / 12.0)


def viscosity_of(energy, rate):
    return base_viscosity + energy / (rate + wall_rate)


def lane_shift(x, amount, fill):
    lane = lax.broadcasted_iota(jnp.int32, x.shape, 1)
    rolled = pltpu.roll(x, (-amount) % CELLS_R, axis=1)
    inside = (lane + amount >= 0) & (lane + amount < CELLS_R)
    return jnp.where(inside, rolled, fill)


def flux(center, up, down, v, v_up, v_down):
    return 0.5 * (v + v_up) * (up - center) - 0.5 * (v + v_down) * (center - down)


class Layer:
    def __init__(self, cells, above, wide, s):
        self.cells, self.above, self.wide, self.s = cells, above, wide, s
        self.v = viscosity_of(self.at(4, 0, 0), self.at(5, 0, 0))
        self.v_side = [
            [viscosity_of(self.at(4, d, 0), self.at(5, d, 0)) for d in (1, -1)],
            [viscosity_of(self.at(4, 0, d), self.at(5, 0, d)) for d in (1, -1)],
            [lane_shift(self.v, d, base_viscosity) for d in (1, -1)],
        ]
        self.centers = [self.at(f, 0, 0) for f in range(6)]

    def at(self, f, ds, dg):
        s = self.s
        if dg != 0:
            return self.wide[f, s, 8 + dg : 16 + dg, :]
        if s + ds < 0:
            return self.above[0, f, 2 + s + ds]
        if s + ds >= CELLS_S:
            return self.above[1, f, s + ds - CELLS_S]
        return self.cells[f, s + ds]

    def around(self, f, d):
        if d == 0:
            return [self.at(f, j, 0) for j in (1, -1, 2, -2)]
        if d == 1:
            return [self.at(f, 0, j) for j in (1, -1, 2, -2)]
        return [lane_shift(self.centers[f], j, 0.0) for j in (1, -1, 2, -2)]

    def diffuse(self, f, near, d):
        return flux(self.centers[f], near[0], near[1], self.v, *self.v_side[d])

    def velocity(self):
        strain = None
        updated = []
        for c in range(3):
            change = -slope(*self.around(3, c))
            for d in range(3):
                near = self.around(c, d)
                gradient = slope(*near)
                square = gradient * gradient
                strain = square if strain is None else strain + square
                change = change - self.centers[d] * gradient
                change = change + self.diffuse(c, near, d)
            updated.append(self.centers[c] + time_step * change)
        return updated, strain

    def turbulence(self, strain):
        k, w = self.centers[4], self.centers[5]
        changes = [
            k / (w + wall_rate) * strain - beta_star * k * w,
            alpha_rate * strain - beta_rate * w * w,
        ]
        updated = []
        for change, f in zip(changes, (4, 5)):
            for d in range(3):
                near = self.around(f, d)
                change = change - self.centers[d] * slope(*near)
                change = change + self.diffuse(f, near, d)
            updated.append(self.centers[f] + time_step * change)
        return updated


def point_tiles(a):
    lane = lax.broadcasted_iota(jnp.int32, (16, 128), 1)
    first = jnp.concatenate([a[0:16, 0:128], a[16:32, 0:128]], axis=1)
    rest = jnp.where(lane < 64, a[0:16, 128:256], a[16:32, 128:256])
    tiles = []
    for h in range(2):
        tiles.append(first[8 * h : 8 * h + 8])
        both = [rest[8 * h : 8 * h + 4], rest[8 * h + 4 : 8 * h + 8]]
        tiles.append(jnp.concatenate(both, axis=1))
    return jnp.concatenate(tiles, axis=0)


def radius_rows(d):
    lane = lax.broadcasted_iota(jnp.int32, (8, 128), 1)
    rest = jnp.concatenate([d[8:12, 0:128], d[8:12, 128:256]], axis=0)
    low = jnp.where(lane < 64, rest, 0.0)
    high = jnp.where(lane < 64, 0.0, rest)
    return jnp.concatenate(
        [
            jnp.concatenate([d[0:8, 0:128], low], axis=1),
            jnp.concatenate([d[0:8, 128:256], high], axis=1),
        ],
        axis=0,
    )


def kernel(
    vel, pre, kin, dis, ids, frac, owner, ftab,
    nv_o, ne_o, nr_o, recvb,
    cells, above, wide, pack, edge, nv, strain_v, turb, ids_v, frac_v, ft, choose, W, lhs, vec,
    acc, disk, four, sendb,
    in_sem, out_sem, hs_sem, hr_sem, gs_sem, gr_sem, as_sem, ar_sem, row_sem, plane_sem,
):
    t = lax.axis_index("stream")
    g = lax.axis_index("girth")
    y = t // RING
    z = lax.rem(t, RING)
    other_t = jnp.where(t < RING, t + RING, t - RING)

    own = [
        pltpu.make_async_copy(vel, cells.at[0:3], in_sem.at[0]),
        pltpu.make_async_copy(pre, cells.at[3], in_sem.at[1]),
        pltpu.make_async_copy(kin, cells.at[4], in_sem.at[2]),
        pltpu.make_async_copy(dis, cells.at[5], in_sem.at[3]),
    ]
    for copy in own:
        copy.start()

    barrier = pltpu.get_barrier_semaphore()

    def plane_peer(across, step):
        turned = g + step
        turned = jnp.where(turned >= GIRTH, turned - GIRTH, turned)
        return (other_t if across else t, turned)

    def ring_peer(i):
        return (y * RING + lax.rem(z + i, RING), g)

    def greet(device):
        pl.semaphore_signal(barrier, inc=1, device_id=device, device_id_type=MESH)

    seam_up = t == RING - 1
    seam_down = t == RING

    @pl.when(seam_up)
    def _():
        greet((t + 1, g))

    @pl.when(seam_down)
    def _():
        greet((t - 1, g))

    core = lax.rem(g, 4)
    edge_up = (core == 3) & (g < GIRTH - 1)
    edge_down = (core == 0) & (g > 0)

    @pl.when(edge_up)
    def _():
        greet((t, g + 1))

    @pl.when(edge_down)
    def _():
        greet((t, g - 1))

    for i in (1, RING - 1):
        greet(ring_peer(i))
    same_x = []
    for step in range(1, 4):
        turned = core + step
        same_x.append((t, g - core + jnp.where(turned >= 4, turned - 4, turned)))
    other_x = [plane_peer(False, 4 * step) for step in range(1, 4)]
    across = plane_peer(True, 0)
    for device in same_x + other_x + [across]:
        greet(device)

    points = []
    for half in range(2):
        rows = pl.ds((half * RING + z) * GIRTH, GIRTH)
        points.append(
            pltpu.make_async_copy(ids.at[rows, :], ids_v.at[half], in_sem.at[4 + half])
        )
        points.append(
            pltpu.make_async_copy(frac.at[:, rows, :], frac_v.at[half], in_sem.at[6 + half])
        )
    points.append(pltpu.make_async_copy(ftab, ft, in_sem.at[8]))

    seam = jnp.where(seam_up | seam_down, 1, 0) + jnp.where(edge_up | edge_down, 1, 0)
    pl.semaphore_wait(barrier, 2 + 3 + 3 + 1 + seam)

    def halo(k):
        if k < 8:
            down = k < 4
            field, place = ((vel, pl.ds(0, 3)), (pre, 3), (kin, 4), (dis, 5))[k % 4]
            layers_of = pl.ds(0, 2) if down else pl.ds(2, 2)
            src = field.at[:, layers_of] if k % 4 == 0 else field.at[layers_of]
            dst = above.at[1 if down else 0, place]
            dev = (t - 1, g) if down else (t + 1, g)
        elif k == 8:
            src, dst, dev = pack.at[0], edge.at[1], (t, g - 1)
        else:
            src, dst, dev = pack.at[1], edge.at[0], (t, g + 1)
        return pltpu.make_async_remote_copy(
            src_ref=src, dst_ref=dst, send_sem=hs_sem.at[k], recv_sem=hr_sem.at[k],
            device_id=dev, device_id_type=MESH,
        )

    sides = (range(0, 4), range(4, 8), range(8, 9), range(9, 10))
    sends = (t > 0, t < STREAM - 1, g > 0, g < GIRTH - 1)
    receives = (sends[1], sends[0], sends[3], sends[2])

    def each(side, there, act):
        @pl.when(there[side])
        def _():
            for k in sides[side]:
                act(halo(k))

    for side in (0, 1):
        each(side, sends, lambda copy: copy.start())
    for copy in own:
        copy.wait()
    for f in range(6):
        for s in range(CELLS_S):
            pack[0, f, 2 * s : 2 * s + 2, :] = cells[f, s, 0:2, :]
            pack[1, f, 2 * s : 2 * s + 2, :] = cells[f, s, 6:8, :]
    for side in (2, 3):
        each(side, sends, lambda copy: copy.start())
    for copy in points:
        copy.start()
    for device in other_x:
        pl.semaphore_signal(row_sem, inc=1, device_id=device, device_id_type=MESH)
    for f in range(6):
        for s in range(CELLS_S):
            wide[f, s, 8:16, :] = cells[f, s]

    @pl.when(t == 0)
    def _():
        above[0] = jnp.zeros((6, 2, 8, CELLS_R), F32)

    @pl.when(t == STREAM - 1)
    def _():
        above[1] = jnp.zeros((6, 2, 8, CELLS_R), F32)

    @pl.when(g == 0)
    def _():
        edge[0] = jnp.zeros((6, 8, CELLS_R), F32)

    @pl.when(g == GIRTH - 1)
    def _():
        edge[1] = jnp.zeros((6, 8, CELLS_R), F32)

    sub8 = lax.broadcasted_iota(jnp.int32, (8, 128), 0)
    lane8 = lax.broadcasted_iota(jnp.int32, (8, 128), 1)

    def sector(s, carry):
        count, place = carry
        mine = jnp.where(owner[s] == g, 1, 0)
        here = (sub8 == s // 8) & (lane8 // WIDTH == lax.rem(s, 8))
        value = jnp.where(mine > 0, count * WIDTH, -AZIMUTHS) + lax.rem(lane8, WIDTH)
        return count + mine, jnp.where(here, value, place)

    _, place = lax.fori_loop(
        0, SECTORS, sector, (jnp.int32(0), jnp.full((8, 128), -AZIMUTHS, jnp.int32))
    )
    row = lax.broadcasted_iota(jnp.int32, (256, 128), 0)
    slot = jnp.where(row < 192, row, row - 64)
    for k in range(8):
        hit = slot == place[k : k + 1, :]
        choose[:, k * 128 : (k + 1) * 128] = jnp.where(hit, 1.0, 0.0).astype(BF16)

    for copy in points:
        copy.wait()
    cid = ids_v[...].reshape(PLANE, AZIMUTHS)
    stream_cell = lax.shift_right_logical(cid, 11)
    girth_cell = lax.shift_right_logical(cid, 8) & 7
    wall_cell = cid & 255
    stack = [wall_cell.astype(F32).astype(BF16), stream_cell.astype(F32).astype(BF16)]
    stack.append(girth_cell.astype(F32).astype(BF16))
    for i in range(3):
        stack.extend(parts_of(frac_v[:, i].reshape(PLANE, AZIMUTHS), 3))
    picked = lax.dot_general(
        jnp.concatenate(stack, axis=0), choose[...], (((1,), (1,)), ((), ())),
        preferred_element_type=F32,
    )
    part = [picked[32 * i : 32 * i + 32] for i in range(12)]
    cell_q, cell_s, cell_g = [point_tiles(part[i]) for i in range(3)]
    f_s, f_g, f_q = [
        point_tiles(part[3 + 3 * i] + part[4 + 3 * i] + part[5 + 3 * i]) for i in range(3)
    ]
    vec[0] = cell_s
    vec[1] = f_s
    vec[2] = cell_g
    vec[3] = f_g
    vec[4] = cell_q
    low_parts = parts_of(1.0 - f_q, 2)
    high_parts = parts_of(f_q, 2)
    vec[5] = low_parts[0].astype(F32)
    vec[6] = low_parts[1].astype(F32)
    vec[7] = high_parts[0].astype(F32)
    vec[8] = high_parts[1].astype(F32)

    chosen = jnp.dot(choose[...], ft[...], preferred_element_type=F32).astype(BF16)
    four[0:256, :] = chosen[:, 0:256]
    four[256:512, :] = chosen[:, 256:512]

    def weights(n, carry):
        def v(i):
            return vec[i, pl.ds(n, 1), :]

        q = lax.broadcasted_iota(jnp.int32, (CELLS_R, 256), 0).astype(F32)
        at_q = q == v(4)
        at_up = q == v(4) + 1.0
        high = jnp.where(at_q, v(5), jnp.where(at_up, v(7), 0.0)).astype(BF16)
        low = jnp.where(at_q, v(6), jnp.where(at_up, v(8), 0.0)).astype(BF16)
        cols = pl.ds(pl.multiple_of(n * 256, 256), 256)
        W[0:256, cols] = high
        W[256:512, cols] = low
        return carry

    lax.fori_loop(0, TILES, weights, 0, unroll=2)
    sendb[...] = jnp.zeros_like(sendb)

    pl.semaphore_wait(row_sem, 3)
    pl.semaphore_signal(plane_sem, inc=1, device_id=across, device_id_type=MESH)

    for side in range(4):
        each(side, receives, lambda copy: copy.wait_recv())
    for f in range(6):
        for s in range(CELLS_S):
            wide[f, s, 6:8, :] = edge[0, f, 2 * s : 2 * s + 2, :]
            wide[f, s, 16:18, :] = edge[1, f, 2 * s : 2 * s + 2, :]

    def gather(i, s):
        return pltpu.make_async_remote_copy(
            src_ref=nv.at[0, s], dst_ref=nv.at[RING - i, s],
            send_sem=gs_sem.at[i * CELLS_S + s], recv_sem=gr_sem.at[i * CELLS_S + s],
            device_id=ring_peer(i), device_id_type=MESH,
        )

    for s in range(CELLS_S):
        updated, strain = Layer(cells, above, wide, s).velocity()
        for c in range(3):
            nv[0, s, c] = updated[c]
        strain_v[s] = strain
        for i in (2, 1, 3):
            gather(i, s).start()
    for s in range(CELLS_S):
        turb[0, s], turb[1, s] = Layer(cells, above, wide, s).turbulence(strain_v[s])
    results = [
        pltpu.make_async_copy(nv.at[0, s], nv_o.at[:, s], out_sem.at[s]) for s in range(CELLS_S)
    ]
    results.append(pltpu.make_async_copy(turb.at[0], ne_o, out_sem.at[4]))
    results.append(pltpu.make_async_copy(turb.at[1], nr_o, out_sem.at[5]))
    for copy in results:
        copy.start()

    def load_blocks(first, count):
        value = jnp.concatenate(
            [nv[first + b].reshape(ROWS, CELLS_R) for b in range(count)], axis=0
        )
        high, low = parts_of(value, 2)
        start = 2 * first * ROWS
        lhs[start : start + count * ROWS, :] = high
        lhs[start + count * ROWS : start + 2 * count * ROWS, :] = low

    def layers(blocks, n, sums):
        first, count = blocks
        start, rows = 2 * first * ROWS, count * ROWS
        cols = pl.ds(pl.multiple_of(n * 256, 256), 256)
        both = jnp.dot(
            lhs[start : start + 2 * rows, :], W[0:256, cols], preferred_element_type=F32
        )
        fine = jnp.dot(lhs[start : start + rows, :], W[256:512, cols], preferred_element_type=F32)
        out = both[0:rows] + both[rows : 2 * rows] + fine
        cell = jnp.broadcast_to(vec[0, pl.ds(n, 1), :], (8, 256))
        up = jnp.broadcast_to(vec[1, pl.ds(n, 1), :], (8, 256))
        stay = 1.0 - up
        for b in range(count):
            base = ((y * RING + lax.rem(z + first + b, RING)) * CELLS_S).astype(F32)
            above_base = cell - base
            for s in range(CELLS_S):
                weight = jnp.where(
                    above_base == s, stay, jnp.where(above_base == s - 1, up, 0.0)
                )
                for c in range(3):
                    at = b * ROWS + s * 24 + c * 8
                    term = weight * out[at : at + 8]
                    sums[c] = term if sums[c] is None else sums[c] + term
        return sums

    load_blocks(0, 1)

    def first_pass(n, carry):
        sums = layers((0, 1), n, [None] * 3)
        for c in range(3):
            acc[c * TILES + n] = sums[c]
        return carry

    lax.fori_loop(0, TILES, first_pass, 0, unroll=4)

    for i in range(1, RING):
        for s in range(CELLS_S):
            gather(i, s).wait_recv()
    load_blocks(1, RING - 1)

    near = g // 8
    column = lax.rem(g, 8)

    def slot_of(i):
        return pl.ds(pl.multiple_of(i * 8, 8), 8)

    def post(turn, j):
        half = 1 - near if turn == 0 else near
        turned = column + j % 8
        turned = jnp.where(turned >= 8, turned - 8, turned)
        across = 1 - y if j >= 8 else y
        dev = (other_t if j >= 8 else t, half * 8 + turned)
        return pltpu.make_async_remote_copy(
            src_ref=sendb.at[slot_of(16 * turn + across * 8 + turned), :],
            dst_ref=recvb.at[pl.ds(8 * (16 * turn + j), 8), :],
            send_sem=as_sem.at[turn], recv_sem=ar_sem.at[turn],
            device_id=dev, device_id_type=MESH,
        )

    def posts(turn):
        span = pl.ds(128 * turn + 8 * turn, 128 - 8 * turn)
        return pltpu.make_async_remote_copy(
            src_ref=sendb.at[span, :], dst_ref=recvb.at[span, :],
            send_sem=as_sem.at[turn], recv_sem=ar_sem.at[turn],
            device_id=plane_peer(True, 0), device_id_type=MESH,
        )

    pl.semaphore_wait(plane_sem, 1)
    for turn in range(2):
        offset = ((1 - near) if turn == 0 else near) * HALF

        def second_pass(k, carry, offset=offset):
            n = offset + k
            sums = layers((1, 3), n, [acc[c * TILES + n] for c in range(3)])
            cell = vec[2, pl.ds(n, 1), :]
            up = vec[3, pl.ds(n, 1), :]
            side = lax.broadcasted_iota(jnp.int32, (8, 256), 0).astype(F32)
            weight = jnp.where(side == cell, 1.0 - up, jnp.where(side == cell + 1.0, up, 0.0))
            for c in range(3):
                disk[pl.ds(c * 16 + k, 1), :] = jnp.sum(sums[c] * weight, axis=0, keepdims=True)
            return carry

        lax.fori_loop(0, HALF, second_pass, 0, unroll=12)
        rows = jnp.concatenate(
            [radius_rows(disk[c * 16 : c * 16 + HALF, :]) for c in range(3)], axis=0
        )
        high, low = parts_of(rows, 2)
        both = jnp.dot(
            jnp.concatenate([high, low], axis=0), four[0:256, :], preferred_element_type=F32
        )
        fine = jnp.dot(high, four[256:512, :], preferred_element_type=F32)
        spectrum = both[0:48] + both[48:96] + fine
        for c in range(3):
            for k in range(2):
                sendb[pl.ds(128 * turn + 2 * c + k, 16, stride=8), :] = spectrum[
                    c * 16 : (c + 1) * 16, k * 128 : (k + 1) * 128
                ]

        for j in range(15, turn - 1, -1):
            post(turn, j).start()

    mine = pltpu.make_async_copy(
        sendb.at[slot_of(16 + y * 8 + column), :], recvb.at[pl.ds(128, 8), :], out_sem.at[6]
    )
    mine.start()
    results.append(mine)
    for side in range(4):
        each(side, sends, lambda copy: copy.wait_send())
    for i in range(1, RING):
        for s in range(CELLS_S):
            gather(i, s).wait_send()
    for copy in results:
        copy.wait()
    for turn in range(2):
        posts(turn).wait_send()
        posts(turn).wait_recv()


def place_results(nv, ne, nr, parts, nv_o, ne_o, nr_o, harm_o):
    nv_o[...] = nv[...]
    ne_o[...] = ne[...]
    nr_o[...] = nr[...]
    total = jnp.sum(parts[...].reshape(PLANE, 8, 128), axis=0)
    for k in range(6):
        harm_o[0:1, k * 128 : (k + 1) * 128] = total[k : k + 1, :]


def body(velocity, pressure, kinetic_energy, dissipation_rate, corner_ids, fractions, sector_owner):
    hbm = pl.BlockSpec(memory_space=pltpu.HBM)
    vmem = pl.BlockSpec(memory_space=pltpu.VMEM)
    smem = pl.BlockSpec(memory_space=pltpu.SMEM)
    dma = pltpu.SemaphoreType.DMA
    shapes = (
        jax.ShapeDtypeStruct(velocity.shape, F32),
        jax.ShapeDtypeStruct(pressure.shape, F32),
        jax.ShapeDtypeStruct(pressure.shape, F32),
        jax.ShapeDtypeStruct((1, 6 * MODES), F32),
    )
    results = pl.pallas_call(
        kernel,
        out_shape=shapes[:3] + (jax.ShapeDtypeStruct((PLANE * 8, 128), F32),),
        in_specs=[hbm] * 6 + [smem, hbm],
        out_specs=(hbm,) * 4,
        scratch_shapes=[
            pltpu.VMEM((6, CELLS_S, CELLS_G, CELLS_R), F32),
            pltpu.VMEM((2, 6, 2, CELLS_G, CELLS_R), F32),
            pltpu.VMEM((6, CELLS_S, 24, CELLS_R), F32),
            pltpu.VMEM((2, 6, 8, CELLS_R), F32),
            pltpu.VMEM((2, 6, 8, CELLS_R), F32),
            pltpu.VMEM((RING, CELLS_S, 3, CELLS_G, CELLS_R), F32),
            pltpu.VMEM((CELLS_S, CELLS_G, CELLS_R), F32),
            pltpu.VMEM((2, CELLS_S, CELLS_G, CELLS_R), F32),
            pltpu.VMEM((2, GIRTH, AZIMUTHS), jnp.int32),
            pltpu.VMEM((2, 3, GIRTH, AZIMUTHS), F32),
            pltpu.VMEM((AZIMUTHS, 512), BF16),
            pltpu.VMEM((256, AZIMUTHS), BF16),
            pltpu.VMEM((512, TILES * 256), BF16),
            pltpu.VMEM((2 * RING * ROWS, 256), BF16),
            pltpu.VMEM((9, TILES, 256), F32),
            pltpu.VMEM((3 * TILES, 8, 256), F32),
            pltpu.VMEM((48, 256), F32),
            pltpu.VMEM((512, 256), BF16),
            pltpu.VMEM((PLANE * 8, 128), F32),
            dma((9,)),
            dma((7,)),
            dma((10,)),
            dma((10,)),
            dma((RING * CELLS_S,)),
            dma((RING * CELLS_S,)),
            dma((2,)),
            dma((2,)),
            pltpu.SemaphoreType.REGULAR,
            pltpu.SemaphoreType.REGULAR,
        ],
        compiler_params=pltpu.CompilerParams(
            collective_id=0, has_side_effects=True, vmem_limit_bytes=VMEM_BYTES
        ),
    )(
        velocity, pressure, kinetic_energy, dissipation_rate, corner_ids, fractions,
        sector_owner.reshape(SECTORS), jnp.asarray(fourier_parts()),
    )
    return pl.pallas_call(
        place_results,
        out_shape=shapes,
        in_specs=[vmem] * 4,
        out_specs=(vmem,) * 4,
        compiler_params=pltpu.CompilerParams(vmem_limit_bytes=VMEM_BYTES),
    )(*results)


def solution(mesh):
    return jax.shard_map(
        body,
        mesh=mesh,
        in_specs=(
            P(None, "stream", "girth", None),
            P("stream", "girth", None),
            P("stream", "girth", None),
            P("stream", "girth", None),
            P(),
            P(),
            P(),
        ),
        out_specs=(
            P(None, "stream", "girth", None),
            P("stream", "girth", None),
            P("stream", "girth", None),
            P(("stream", "girth"), None),
        ),
        check_vma=False,
    )
```

```python
import functools
import math

import jax
import jax.numpy as jnp
import numpy as np
from jax import lax
from jax.experimental import pallas as pl
from jax.experimental.pallas import tpu as pltpu
from jax.sharding import PartitionSpec as P

F32 = jnp.float32
BF16 = jnp.bfloat16
MESH = pl.DeviceIdType.MESH

base_viscosity = 0.05
time_step = 0.2
beta_star = 0.09
beta_rate = 0.075
alpha_rate = 0.52
wall_rate = 1.0

STREAM = 8
GIRTH = 16
RING = 4
PLANE = 32
CELLS_S = 4
CELLS_G = 8
CELLS_R = 256
AZIMUTHS = 1024
MODES = 128
SECTORS = 64
WIDTH = 16
ROWS = 3 * CELLS_S * CELLS_G
TILES = 24
HALF = TILES // 2
VMEM_BYTES = 64 * 1024 * 1024


def fourier_parts():
    a = np.arange(AZIMUTHS)[:, None]
    h = np.arange(MODES)[None, :]
    angle = (a * h % AZIMUTHS) * (2.0 * math.pi / AZIMUTHS)
    table = np.concatenate([np.cos(angle), -np.sin(angle)], axis=1) / math.sqrt(AZIMUTHS)
    table = table.astype(np.float32)
    high = table.astype(jnp.bfloat16)
    low = (table - high.astype(np.float32)).astype(jnp.bfloat16)
    return np.concatenate([high, low], axis=1)


def parts_of(x, count):
    parts = []
    for _ in range(count):
        part = x.astype(BF16)
        parts.append(part)
        x = x - part.astype(F32)
    return parts


def slope(up1, down1, up2, down2):
    return (8.0 * (up1 - down1) - (up2 - down2)) * (1.0 / 12.0)


def viscosity_of(energy, rate):
    return base_viscosity + energy / (rate + wall_rate)


def lane_shift(x, amount, fill):
    lane = lax.broadcasted_iota(jnp.int32, x.shape, 1)
    rolled = pltpu.roll(x, (-amount) % CELLS_R, axis=1)
    inside = (lane + amount >= 0) & (lane + amount < CELLS_R)
    return jnp.where(inside, rolled, fill)


def flux(center, up, down, v, v_up, v_down):
    return 0.5 * (v + v_up) * (up - center) - 0.5 * (v + v_down) * (center - down)


class Layer:
    def __init__(self, cells, above, wide, s):
        self.cells, self.above, self.wide, self.s = cells, above, wide, s
        self.v = viscosity_of(self.at(4, 0, 0), self.at(5, 0, 0))
        self.v_side = [
            [viscosity_of(self.at(4, d, 0), self.at(5, d, 0)) for d in (1, -1)],
            [viscosity_of(self.at(4, 0, d), self.at(5, 0, d)) for d in (1, -1)],
            [lane_shift(self.v, d, base_viscosity) for d in (1, -1)],
        ]
        self.centers = [self.at(f, 0, 0) for f in range(6)]

    def at(self, f, ds, dg):
        s = self.s
        if dg != 0:
            return self.wide[f, s, 8 + dg : 16 + dg, :]
        if s + ds < 0:
            return self.above[0, f, 2 + s + ds]
        if s + ds >= CELLS_S:
            return self.above[1, f, s + ds - CELLS_S]
        return self.cells[f, s + ds]

    def around(self, f, d):
        if d == 0:
            return [self.at(f, j, 0) for j in (1, -1, 2, -2)]
        if d == 1:
            return [self.at(f, 0, j) for j in (1, -1, 2, -2)]
        return [lane_shift(self.centers[f], j, 0.0) for j in (1, -1, 2, -2)]

    def diffuse(self, f, near, d):
        return flux(self.centers[f], near[0], near[1], self.v, *self.v_side[d])

    def velocity(self):
        strain = None
        updated = []
        for c in range(3):
            change = -slope(*self.around(3, c))
            for d in range(3):
                near = self.around(c, d)
                gradient = slope(*near)
                square = gradient * gradient
                strain = square if strain is None else strain + square
                change = change - self.centers[d] * gradient
                change = change + self.diffuse(c, near, d)
            updated.append(self.centers[c] + time_step * change)
        return updated, strain

    def turbulence(self, strain):
        k, w = self.centers[4], self.centers[5]
        changes = [
            k / (w + wall_rate) * strain - beta_star * k * w,
            alpha_rate * strain - beta_rate * w * w,
        ]
        updated = []
        for change, f in zip(changes, (4, 5)):
            for d in range(3):
                near = self.around(f, d)
                change = change - self.centers[d] * slope(*near)
                change = change + self.diffuse(f, near, d)
            updated.append(self.centers[f] + time_step * change)
        return updated


def point_tiles(a):
    lane = lax.broadcasted_iota(jnp.int32, (16, 128), 1)
    first = jnp.concatenate([a[0:16, 0:128], a[16:32, 0:128]], axis=1)
    rest = jnp.where(lane < 64, a[0:16, 128:256], a[16:32, 128:256])
    tiles = []
    for h in range(2):
        tiles.append(first[8 * h : 8 * h + 8])
        both = [rest[8 * h : 8 * h + 4], rest[8 * h + 4 : 8 * h + 8]]
        tiles.append(jnp.concatenate(both, axis=1))
    return jnp.concatenate(tiles, axis=0)


def radius_rows(d):
    lane = lax.broadcasted_iota(jnp.int32, (8, 128), 1)
    rest = jnp.concatenate([d[8:12, 0:128], d[8:12, 128:256]], axis=0)
    low = jnp.where(lane < 64, rest, 0.0)
    high = jnp.where(lane < 64, 0.0, rest)
    return jnp.concatenate(
        [
            jnp.concatenate([d[0:8, 0:128], low], axis=1),
            jnp.concatenate([d[0:8, 128:256], high], axis=1),
        ],
        axis=0,
    )


def kernel(
    vel, pre, kin, dis, ids, frac, owner_in, ftab,
    nv_o, ne_o, nr_o, recvb,
    owner, cells, above, wide, pack, edge, nv, strain_v, turb, ids_v, frac_v, ft, choose, W, lhs, vec,
    acc, disk, four, sendb,
    in_sem, out_sem, hs_sem, hr_sem, gs_sem, gr_sem, as_sem, ar_sem, row_sem, plane_sem,
):
    t = lax.axis_index("stream")
    g = lax.axis_index("girth")
    y = t // RING
    z = lax.rem(t, RING)
    other_t = jnp.where(t < RING, t + RING, t - RING)

    own = [
        pltpu.make_async_copy(vel, cells.at[0:3], in_sem.at[0]),
        pltpu.make_async_copy(pre, cells.at[3], in_sem.at[1]),
        pltpu.make_async_copy(kin, cells.at[4], in_sem.at[2]),
        pltpu.make_async_copy(dis, cells.at[5], in_sem.at[3]),
    ]
    for copy in own:
        copy.start()
    owners = pltpu.make_async_copy(owner_in, owner, in_sem.at[9])
    owners.start()

    barrier = pltpu.get_barrier_semaphore()

    def plane_peer(across, step):
        turned = g + step
        turned = jnp.where(turned >= GIRTH, turned - GIRTH, turned)
        return (other_t if across else t, turned)

    def ring_peer(i):
        return (y * RING + lax.rem(z + i, RING), g)

    def greet(device):
        pl.semaphore_signal(barrier, inc=1, device_id=device, device_id_type=MESH)

    seam_up = t == RING - 1
    seam_down = t == RING

    @pl.when(seam_up)
    def _():
        greet((t + 1, g))

    @pl.when(seam_down)
    def _():
        greet((t - 1, g))

    core = lax.rem(g, 4)
    edge_up = (core == 3) & (g < GIRTH - 1)
    edge_down = (core == 0) & (g > 0)

    @pl.when(edge_up)
    def _():
        greet((t, g + 1))

    @pl.when(edge_down)
    def _():
        greet((t, g - 1))

    for i in (1, RING - 1):
        greet(ring_peer(i))
    same_x = []
    for step in range(1, 4):
        turned = core + step
        same_x.append((t, g - core + jnp.where(turned >= 4, turned - 4, turned)))
    other_x = [plane_peer(False, 4 * step) for step in range(1, 4)]
    across = plane_peer(True, 0)
    for device in same_x + other_x + [across]:
        greet(device)

    points = []
    for half in range(2):
        rows = pl.ds((half * RING + z) * GIRTH, GIRTH)
        points.append(
            pltpu.make_async_copy(ids.at[rows, :], ids_v.at[half], in_sem.at[4 + half])
        )
        points.append(
            pltpu.make_async_copy(frac.at[:, rows, :], frac_v.at[half], in_sem.at[6 + half])
        )
    points.append(pltpu.make_async_copy(ftab, ft, in_sem.at[8]))

    seam = jnp.where(seam_up | seam_down, 1, 0) + jnp.where(edge_up | edge_down, 1, 0)
    pl.semaphore_wait(barrier, 2 + 3 + 3 + 1 + seam)

    def halo(k):
        if k < 8:
            down = k < 4
            field, place = ((vel, pl.ds(0, 3)), (pre, 3), (kin, 4), (dis, 5))[k % 4]
            layers_of = pl.ds(0, 2) if down else pl.ds(2, 2)
            src = field.at[:, layers_of] if k % 4 == 0 else field.at[layers_of]
            dst = above.at[1 if down else 0, place]
            dev = (t - 1, g) if down else (t + 1, g)
        elif k == 8:
            src, dst, dev = pack.at[0], edge.at[1], (t, g - 1)
        else:
            src, dst, dev = pack.at[1], edge.at[0], (t, g + 1)
        return pltpu.make_async_remote_copy(
            src_ref=src, dst_ref=dst, send_sem=hs_sem.at[k], recv_sem=hr_sem.at[k],
            device_id=dev, device_id_type=MESH,
        )

    sides = (range(0, 4), range(4, 8), range(8, 9), range(9, 10))
    sends = (t > 0, t < STREAM - 1, g > 0, g < GIRTH - 1)
    receives = (sends[1], sends[0], sends[3], sends[2])

    def each(side, there, act):
        @pl.when(there[side])
        def _():
            for k in sides[side]:
                act(halo(k))

    for side in (0, 1):
        each(side, sends, lambda copy: copy.start())
    for copy in own:
        copy.wait()
    for f in range(6):
        for s in range(CELLS_S):
            pack[0, f, 2 * s : 2 * s + 2, :] = cells[f, s, 0:2, :]
            pack[1, f, 2 * s : 2 * s + 2, :] = cells[f, s, 6:8, :]
    for side in (2, 3):
        each(side, sends, lambda copy: copy.start())
    for copy in points:
        copy.start()
    for device in other_x:
        pl.semaphore_signal(row_sem, inc=1, device_id=device, device_id_type=MESH)
    for f in range(6):
        for s in range(CELLS_S):
            wide[f, s, 8:16, :] = cells[f, s]

    @pl.when(t == 0)
    def _():
        above[0] = jnp.zeros((6, 2, 8, CELLS_R), F32)

    @pl.when(t == STREAM - 1)
    def _():
        above[1] = jnp.zeros((6, 2, 8, CELLS_R), F32)

    @pl.when(g == 0)
    def _():
        edge[0] = jnp.zeros((6, 8, CELLS_R), F32)

    @pl.when(g == GIRTH - 1)
    def _():
        edge[1] = jnp.zeros((6, 8, CELLS_R), F32)

    sub8 = lax.broadcasted_iota(jnp.int32, (8, 128), 0)
    lane8 = lax.broadcasted_iota(jnp.int32, (8, 128), 1)

    def sector(s, carry):
        count, place = carry
        mine = jnp.where(owner[s] == g, 1, 0)
        here = (sub8 == s // 8) & (lane8 // WIDTH == lax.rem(s, 8))
        value = jnp.where(mine > 0, count * WIDTH, -AZIMUTHS) + lax.rem(lane8, WIDTH)
        return count + mine, jnp.where(here, value, place)

    owners.wait()
    _, place = lax.fori_loop(
        0, SECTORS, sector, (jnp.int32(0), jnp.full((8, 128), -AZIMUTHS, jnp.int32))
    )
    row = lax.broadcasted_iota(jnp.int32, (256, 128), 0)
    slot = jnp.where(row < 192, row, row - 64)
    for k in range(8):
        hit = slot == place[k : k + 1, :]
        choose[:, k * 128 : (k + 1) * 128] = jnp.where(hit, 1.0, 0.0).astype(BF16)

    for copy in points:
        copy.wait()
    cid = ids_v[...].reshape(PLANE, AZIMUTHS)
    stream_cell = lax.shift_right_logical(cid, 11)
    girth_cell = lax.shift_right_logical(cid, 8) & 7
    wall_cell = cid & 255
    stack = [wall_cell.astype(F32).astype(BF16), stream_cell.astype(F32).astype(BF16)]
    stack.append(girth_cell.astype(F32).astype(BF16))
    for i in range(3):
        stack.extend(parts_of(frac_v[:, i].reshape(PLANE, AZIMUTHS), 3))
    picked = lax.dot_general(
        jnp.concatenate(stack, axis=0), choose[...], (((1,), (1,)), ((), ())),
        preferred_element_type=F32,
    )
    part = [picked[32 * i : 32 * i + 32] for i in range(12)]
    cell_q, cell_s, cell_g = [point_tiles(part[i]) for i in range(3)]
    f_s, f_g, f_q = [
        point_tiles(part[3 + 3 * i] + part[4 + 3 * i] + part[5 + 3 * i]) for i in range(3)
    ]
    vec[0] = cell_s
    vec[1] = f_s
    vec[2] = cell_g
    vec[3] = f_g
    vec[4] = cell_q
    low_parts = parts_of(1.0 - f_q, 2)
    high_parts = parts_of(f_q, 2)
    vec[5] = low_parts[0].astype(F32)
    vec[6] = low_parts[1].astype(F32)
    vec[7] = high_parts[0].astype(F32)
    vec[8] = high_parts[1].astype(F32)

    chosen = jnp.dot(choose[...], ft[...], preferred_element_type=F32).astype(BF16)
    four[0:256, :] = chosen[:, 0:256]
    four[256:512, :] = chosen[:, 256:512]

    def weights(n, carry):
        def v(i):
            return vec[i, pl.ds(n, 1), :]

        q = lax.broadcasted_iota(jnp.int32, (CELLS_R, 256), 0).astype(F32)
        at_q = q == v(4)
        at_up = q == v(4) + 1.0
        high = jnp.where(at_q, v(5), jnp.where(at_up, v(7), 0.0)).astype(BF16)
        low = jnp.where(at_q, v(6), jnp.where(at_up, v(8), 0.0)).astype(BF16)
        cols = pl.ds(pl.multiple_of(n * 256, 256), 256)
        W[0:256, cols] = high
        W[256:512, cols] = low
        return carry

    lax.fori_loop(0, TILES, weights, 0, unroll=2)
    sendb[...] = jnp.zeros_like(sendb)

    pl.semaphore_wait(row_sem, 3)
    pl.semaphore_signal(plane_sem, inc=1, device_id=across, device_id_type=MESH)

    for side in range(4):
        each(side, receives, lambda copy: copy.wait_recv())
    for f in range(6):
        for s in range(CELLS_S):
            wide[f, s, 6:8, :] = edge[0, f, 2 * s : 2 * s + 2, :]
            wide[f, s, 16:18, :] = edge[1, f, 2 * s : 2 * s + 2, :]

    def gather(i, s):
        return pltpu.make_async_remote_copy(
            src_ref=nv.at[0, s], dst_ref=nv.at[RING - i, s],
            send_sem=gs_sem.at[i * CELLS_S + s], recv_sem=gr_sem.at[i * CELLS_S + s],
            device_id=ring_peer(i), device_id_type=MESH,
        )

    for s in range(CELLS_S):
        updated, strain = Layer(cells, above, wide, s).velocity()
        for c in range(3):
            nv[0, s, c] = updated[c]
        strain_v[s] = strain
        for i in (2, 1, 3):
            gather(i, s).start()
    for s in range(CELLS_S):
        turb[0, s], turb[1, s] = Layer(cells, above, wide, s).turbulence(strain_v[s])
    results = [
        pltpu.make_async_copy(nv.at[0, s], nv_o.at[:, s], out_sem.at[s]) for s in range(CELLS_S)
    ]
    results.append(pltpu.make_async_copy(turb.at[0], ne_o, out_sem.at[4]))
    results.append(pltpu.make_async_copy(turb.at[1], nr_o, out_sem.at[5]))
    for copy in results:
        copy.start()

    def load_blocks(first, count):
        value = jnp.concatenate(
            [nv[first + b].reshape(ROWS, CELLS_R) for b in range(count)], axis=0
        )
        high, low = parts_of(value, 2)
        start = 2 * first * ROWS
        lhs[start : start + count * ROWS, :] = high
        lhs[start + count * ROWS : start + 2 * count * ROWS, :] = low

    def layers(blocks, n, sums):
        first, count = blocks
        start, rows = 2 * first * ROWS, count * ROWS
        cols = pl.ds(pl.multiple_of(n * 256, 256), 256)
        both = jnp.dot(
            lhs[start : start + 2 * rows, :], W[0:256, cols], preferred_element_type=F32
        )
        fine = jnp.dot(lhs[start : start + rows, :], W[256:512, cols], preferred_element_type=F32)
        out = both[0:rows] + both[rows : 2 * rows] + fine
        cell = jnp.broadcast_to(vec[0, pl.ds(n, 1), :], (8, 256))
        up = jnp.broadcast_to(vec[1, pl.ds(n, 1), :], (8, 256))
        stay = 1.0 - up
        for b in range(count):
            base = ((y * RING + lax.rem(z + first + b, RING)) * CELLS_S).astype(F32)
            above_base = cell - base
            for s in range(CELLS_S):
                weight = jnp.where(
                    above_base == s, stay, jnp.where(above_base == s - 1, up, 0.0)
                )
                for c in range(3):
                    at = b * ROWS + s * 24 + c * 8
                    term = weight * out[at : at + 8]
                    sums[c] = term if sums[c] is None else sums[c] + term
        return sums

    load_blocks(0, 1)

    def first_pass(n, carry):
        sums = layers((0, 1), n, [None] * 3)
        for c in range(3):
            acc[c * TILES + n] = sums[c]
        return carry

    lax.fori_loop(0, TILES, first_pass, 0, unroll=4)

    for i in range(1, RING):
        for s in range(CELLS_S):
            gather(i, s).wait_recv()
    load_blocks(1, RING - 1)

    near = g // 8
    column = lax.rem(g, 8)

    def slot_of(i):
        return pl.ds(pl.multiple_of(i * 8, 8), 8)

    def post(turn, j):
        half = 1 - near if turn == 0 else near
        turned = column + j % 8
        turned = jnp.where(turned >= 8, turned - 8, turned)
        across = 1 - y if j >= 8 else y
        dev = (other_t if j >= 8 else t, half * 8 + turned)
        return pltpu.make_async_remote_copy(
            src_ref=sendb.at[slot_of(16 * turn + across * 8 + turned), :],
            dst_ref=recvb.at[pl.ds(8 * (16 * turn + j), 8), :],
            send_sem=as_sem.at[turn], recv_sem=ar_sem.at[turn],
            device_id=dev, device_id_type=MESH,
        )

    def posts(turn):
        span = pl.ds(128 * turn + 8 * turn, 128 - 8 * turn)
        return pltpu.make_async_remote_copy(
            src_ref=sendb.at[span, :], dst_ref=recvb.at[span, :],
            send_sem=as_sem.at[turn], recv_sem=ar_sem.at[turn],
            device_id=plane_peer(True, 0), device_id_type=MESH,
        )

    pl.semaphore_wait(plane_sem, 1)
    for turn in range(2):
        offset = ((1 - near) if turn == 0 else near) * HALF

        def second_pass(k, carry, offset=offset):
            n = offset + k
            sums = layers((1, 3), n, [acc[c * TILES + n] for c in range(3)])
            cell = vec[2, pl.ds(n, 1), :]
            up = vec[3, pl.ds(n, 1), :]
            side = lax.broadcasted_iota(jnp.int32, (8, 256), 0).astype(F32)
            weight = jnp.where(side == cell, 1.0 - up, jnp.where(side == cell + 1.0, up, 0.0))
            for c in range(3):
                disk[pl.ds(c * 16 + k, 1), :] = jnp.sum(sums[c] * weight, axis=0, keepdims=True)
            return carry

        lax.fori_loop(0, HALF, second_pass, 0, unroll=12)
        rows = jnp.concatenate(
            [radius_rows(disk[c * 16 : c * 16 + HALF, :]) for c in range(3)], axis=0
        )
        high, low = parts_of(rows, 2)
        both = jnp.dot(
            jnp.concatenate([high, low], axis=0), four[0:256, :], preferred_element_type=F32
        )
        fine = jnp.dot(high, four[256:512, :], preferred_element_type=F32)
        spectrum = both[0:48] + both[48:96] + fine
        for c in range(3):
            for k in range(2):
                sendb[pl.ds(128 * turn + 2 * c + k, 16, stride=8), :] = spectrum[
                    c * 16 : (c + 1) * 16, k * 128 : (k + 1) * 128
                ]

        for j in range(15, turn - 1, -1):
            post(turn, j).start()

    mine = pltpu.make_async_copy(
        sendb.at[slot_of(16 + y * 8 + column), :], recvb.at[pl.ds(128, 8), :], out_sem.at[6]
    )
    mine.start()
    results.append(mine)
    for side in range(4):
        each(side, sends, lambda copy: copy.wait_send())
    for i in range(1, RING):
        for s in range(CELLS_S):
            gather(i, s).wait_send()
    for copy in results:
        copy.wait()
    for turn in range(2):
        posts(turn).wait_send()
        posts(turn).wait_recv()


def place_results(nv, ne, nr, parts, nv_o, ne_o, nr_o, harm_o):
    nv_o[...] = nv[...]
    ne_o[...] = ne[...]
    nr_o[...] = nr[...]
    total = jnp.sum(parts[...].reshape(PLANE, 8, 128), axis=0)
    for k in range(6):
        harm_o[0:1, k * 128 : (k + 1) * 128] = total[k : k + 1, :]


def body(velocity, pressure, kinetic_energy, dissipation_rate, corner_ids, fractions, sector_owner):
    hbm = pl.BlockSpec(memory_space=pltpu.HBM)
    vmem = pl.BlockSpec(memory_space=pltpu.VMEM)
    dma = pltpu.SemaphoreType.DMA
    shapes = (
        jax.ShapeDtypeStruct(velocity.shape, F32),
        jax.ShapeDtypeStruct(pressure.shape, F32),
        jax.ShapeDtypeStruct(pressure.shape, F32),
        jax.ShapeDtypeStruct((1, 6 * MODES), F32),
    )
    results = pl.pallas_call(
        kernel,
        out_shape=shapes[:3] + (jax.ShapeDtypeStruct((PLANE * 8, 128), F32),),
        in_specs=[hbm] * 8,
        out_specs=(hbm,) * 4,
        scratch_shapes=[
            pltpu.SMEM((SECTORS,), jnp.int32),
            pltpu.VMEM((6, CELLS_S, CELLS_G, CELLS_R), F32),
            pltpu.VMEM((2, 6, 2, CELLS_G, CELLS_R), F32),
            pltpu.VMEM((6, CELLS_S, 24, CELLS_R), F32),
            pltpu.VMEM((2, 6, 8, CELLS_R), F32),
            pltpu.VMEM((2, 6, 8, CELLS_R), F32),
            pltpu.VMEM((RING, CELLS_S, 3, CELLS_G, CELLS_R), F32),
            pltpu.VMEM((CELLS_S, CELLS_G, CELLS_R), F32),
            pltpu.VMEM((2, CELLS_S, CELLS_G, CELLS_R), F32),
            pltpu.VMEM((2, GIRTH, AZIMUTHS), jnp.int32),
            pltpu.VMEM((2, 3, GIRTH, AZIMUTHS), F32),
            pltpu.VMEM((AZIMUTHS, 512), BF16),
            pltpu.VMEM((256, AZIMUTHS), BF16),
            pltpu.VMEM((512, TILES * 256), BF16),
            pltpu.VMEM((2 * RING * ROWS, 256), BF16),
            pltpu.VMEM((9, TILES, 256), F32),
            pltpu.VMEM((3 * TILES, 8, 256), F32),
            pltpu.VMEM((48, 256), F32),
            pltpu.VMEM((512, 256), BF16),
            pltpu.VMEM((PLANE * 8, 128), F32),
            dma((10,)),
            dma((7,)),
            dma((10,)),
            dma((10,)),
            dma((RING * CELLS_S,)),
            dma((RING * CELLS_S,)),
            dma((2,)),
            dma((2,)),
            pltpu.SemaphoreType.REGULAR,
            pltpu.SemaphoreType.REGULAR,
        ],
        compiler_params=pltpu.CompilerParams(
            collective_id=0, has_side_effects=True, vmem_limit_bytes=VMEM_BYTES
        ),
    )(
        velocity, pressure, kinetic_energy, dissipation_rate, corner_ids, fractions,
        sector_owner.reshape(SECTORS), jnp.asarray(fourier_parts()),
    )
    return pl.pallas_call(
        place_results,
        out_shape=shapes,
        in_specs=[vmem] * 4,
        out_specs=(vmem,) * 4,
        compiler_params=pltpu.CompilerParams(vmem_limit_bytes=VMEM_BYTES),
    )(*results)


def solution(mesh):
    return jax.shard_map(
        body,
        mesh=mesh,
        in_specs=(
            P(None, "stream", "girth", None),
            P("stream", "girth", None),
            P("stream", "girth", None),
            P("stream", "girth", None),
            P(),
            P(),
            P(),
        ),
        out_specs=(
            P(None, "stream", "girth", None),
            P("stream", "girth", None),
            P("stream", "girth", None),
            P(("stream", "girth"), None),
        ),
        check_vma=False,
    )
```

```python
import functools
import math

import jax
import jax.numpy as jnp
import numpy as np
from jax import lax
from jax.experimental import pallas as pl
from jax.experimental.pallas import tpu as pltpu
from jax.sharding import PartitionSpec as P

F32 = jnp.float32
BF16 = jnp.bfloat16
MESH = pl.DeviceIdType.MESH

base_viscosity = 0.05
time_step = 0.2
beta_star = 0.09
beta_rate = 0.075
alpha_rate = 0.52
wall_rate = 1.0

STREAM = 8
GIRTH = 16
RING = 4
PLANE = 32
CELLS_S = 4
CELLS_G = 8
CELLS_R = 256
AZIMUTHS = 1024
MODES = 128
SECTORS = 64
WIDTH = 16
ROWS = 3 * CELLS_S * CELLS_G
TILES = 24
HALF = TILES // 2
VMEM_BYTES = 64 * 1024 * 1024


def fourier_parts():
    a = np.arange(AZIMUTHS)[:, None]
    h = np.arange(MODES)[None, :]
    angle = (a * h % AZIMUTHS) * (2.0 * math.pi / AZIMUTHS)
    table = np.concatenate([np.cos(angle), -np.sin(angle)], axis=1) / math.sqrt(AZIMUTHS)
    table = table.astype(np.float32)
    high = table.astype(jnp.bfloat16)
    low = (table - high.astype(np.float32)).astype(jnp.bfloat16)
    return np.concatenate([high, low], axis=1)


def parts_of(x, count):
    parts = []
    for _ in range(count):
        part = x.astype(BF16)
        parts.append(part)
        x = x - part.astype(F32)
    return parts


def slope(up1, down1, up2, down2):
    return (8.0 * (up1 - down1) - (up2 - down2)) * (1.0 / 12.0)


def viscosity_of(energy, rate):
    return base_viscosity + energy / (rate + wall_rate)


def lane_shift(x, amount, fill):
    lane = lax.broadcasted_iota(jnp.int32, x.shape, 1)
    rolled = pltpu.roll(x, (-amount) % CELLS_R, axis=1)
    inside = (lane + amount >= 0) & (lane + amount < CELLS_R)
    return jnp.where(inside, rolled, fill)


def flux(center, up, down, v, v_up, v_down):
    return 0.5 * (v + v_up) * (up - center) - 0.5 * (v + v_down) * (center - down)


class Layer:
    def __init__(self, cells, above, wide, s):
        self.cells, self.above, self.wide, self.s = cells, above, wide, s
        self.v = viscosity_of(self.at(4, 0, 0), self.at(5, 0, 0))
        self.v_side = [
            [viscosity_of(self.at(4, d, 0), self.at(5, d, 0)) for d in (1, -1)],
            [viscosity_of(self.at(4, 0, d), self.at(5, 0, d)) for d in (1, -1)],
            [lane_shift(self.v, d, base_viscosity) for d in (1, -1)],
        ]
        self.centers = [self.at(f, 0, 0) for f in range(6)]

    def at(self, f, ds, dg):
        s = self.s
        if dg != 0:
            return self.wide[f, s, 8 + dg : 16 + dg, :]
        if s + ds < 0:
            return self.above[0, f, 2 + s + ds]
        if s + ds >= CELLS_S:
            return self.above[1, f, s + ds - CELLS_S]
        return self.cells[f, s + ds]

    def around(self, f, d):
        if d == 0:
            return [self.at(f, j, 0) for j in (1, -1, 2, -2)]
        if d == 1:
            return [self.at(f, 0, j) for j in (1, -1, 2, -2)]
        return [lane_shift(self.centers[f], j, 0.0) for j in (1, -1, 2, -2)]

    def diffuse(self, f, near, d):
        return flux(self.centers[f], near[0], near[1], self.v, *self.v_side[d])

    def velocity(self):
        strain = None
        updated = []
        for c in range(3):
            change = -slope(*self.around(3, c))
            for d in range(3):
                near = self.around(c, d)
                gradient = slope(*near)
                square = gradient * gradient
                strain = square if strain is None else strain + square
                change = change - self.centers[d] * gradient
                change = change + self.diffuse(c, near, d)
            updated.append(self.centers[c] + time_step * change)
        return updated, strain

    def turbulence(self, strain):
        k, w = self.centers[4], self.centers[5]
        changes = [
            k / (w + wall_rate) * strain - beta_star * k * w,
            alpha_rate * strain - beta_rate * w * w,
        ]
        updated = []
        for change, f in zip(changes, (4, 5)):
            for d in range(3):
                near = self.around(f, d)
                change = change - self.centers[d] * slope(*near)
                change = change + self.diffuse(f, near, d)
            updated.append(self.centers[f] + time_step * change)
        return updated


def point_tiles(a):
    lane = lax.broadcasted_iota(jnp.int32, (16, 128), 1)
    first = jnp.concatenate([a[0:16, 0:128], a[16:32, 0:128]], axis=1)
    rest = jnp.where(lane < 64, a[0:16, 128:256], a[16:32, 128:256])
    tiles = []
    for h in range(2):
        tiles.append(first[8 * h : 8 * h + 8])
        both = [rest[8 * h : 8 * h + 4], rest[8 * h + 4 : 8 * h + 8]]
        tiles.append(jnp.concatenate(both, axis=1))
    return jnp.concatenate(tiles, axis=0)


def radius_rows(d):
    lane = lax.broadcasted_iota(jnp.int32, (8, 128), 1)
    rest = jnp.concatenate([d[8:12, 0:128], d[8:12, 128:256]], axis=0)
    low = jnp.where(lane < 64, rest, 0.0)
    high = jnp.where(lane < 64, 0.0, rest)
    return jnp.concatenate(
        [
            jnp.concatenate([d[0:8, 0:128], low], axis=1),
            jnp.concatenate([d[0:8, 128:256], high], axis=1),
        ],
        axis=0,
    )


def kernel(
    vel, pre, kin, dis, ids, frac, owner_in, ftab,
    nv_o, ne_o, nr_o, recvb,
    owner, cells, above, wide, pack, edge, nv, strain_v, turb, ids_v, frac_v, ft, choose, W, lhs, vec,
    acc, disk, four, sendb,
    in_sem, out_sem, hs_sem, hr_sem, gs_sem, gr_sem, as_sem, ar_sem, row_sem, plane_sem,
):
    t = lax.axis_index("stream")
    g = lax.axis_index("girth")
    y = t // RING
    z = lax.rem(t, RING)
    other_t = jnp.where(t < RING, t + RING, t - RING)

    own = [
        pltpu.make_async_copy(vel, cells.at[0:3], in_sem.at[0]),
        pltpu.make_async_copy(pre, cells.at[3], in_sem.at[1]),
        pltpu.make_async_copy(kin, cells.at[4], in_sem.at[2]),
        pltpu.make_async_copy(dis, cells.at[5], in_sem.at[3]),
    ]
    owners = pltpu.make_async_copy(owner_in, owner, in_sem.at[9])
    barrier = pltpu.get_barrier_semaphore()

    def plane_peer(across, step):
        turned = g + step
        turned = jnp.where(turned >= GIRTH, turned - GIRTH, turned)
        return (other_t if across else t, turned)

    def ring_peer(i):
        return (y * RING + lax.rem(z + i, RING), g)

    def greet(device):
        pl.semaphore_signal(barrier, inc=1, device_id=device, device_id_type=MESH)

    seam_up = t == RING - 1
    seam_down = t == RING

    @pl.when(seam_up)
    def _():
        greet((t + 1, g))

    @pl.when(seam_down)
    def _():
        greet((t - 1, g))

    core = lax.rem(g, 4)
    edge_up = (core == 3) & (g < GIRTH - 1)
    edge_down = (core == 0) & (g > 0)

    @pl.when(edge_up)
    def _():
        greet((t, g + 1))

    @pl.when(edge_down)
    def _():
        greet((t, g - 1))

    for i in (1, RING - 1):
        greet(ring_peer(i))
    same_x = []
    for step in range(1, 4):
        turned = core + step
        same_x.append((t, g - core + jnp.where(turned >= 4, turned - 4, turned)))
    other_x = [plane_peer(False, 4 * step) for step in range(1, 4)]
    across = plane_peer(True, 0)
    for device in same_x + other_x + [across]:
        greet(device)

    for copy in own:
        copy.start()
    points = []
    for half in range(2):
        rows = pl.ds((half * RING + z) * GIRTH, GIRTH)
        points.append(
            pltpu.make_async_copy(ids.at[rows, :], ids_v.at[half], in_sem.at[4 + half])
        )
        points.append(
            pltpu.make_async_copy(frac.at[:, rows, :], frac_v.at[half], in_sem.at[6 + half])
        )
    points.append(pltpu.make_async_copy(ftab, ft, in_sem.at[8]))

    seam = jnp.where(seam_up | seam_down, 1, 0) + jnp.where(edge_up | edge_down, 1, 0)
    pl.semaphore_wait(barrier, 2 + 3 + 3 + 1 + seam)

    def halo(k):
        if k < 8:
            down = k < 4
            field, place = ((vel, pl.ds(0, 3)), (pre, 3), (kin, 4), (dis, 5))[k % 4]
            layers_of = pl.ds(0, 2) if down else pl.ds(2, 2)
            src = field.at[:, layers_of] if k % 4 == 0 else field.at[layers_of]
            dst = above.at[1 if down else 0, place]
            dev = (t - 1, g) if down else (t + 1, g)
        elif k == 8:
            src, dst, dev = pack.at[0], edge.at[1], (t, g - 1)
        else:
            src, dst, dev = pack.at[1], edge.at[0], (t, g + 1)
        return pltpu.make_async_remote_copy(
            src_ref=src, dst_ref=dst, send_sem=hs_sem.at[k], recv_sem=hr_sem.at[k],
            device_id=dev, device_id_type=MESH,
        )

    sides = (range(0, 4), range(4, 8), range(8, 9), range(9, 10))
    sends = (t > 0, t < STREAM - 1, g > 0, g < GIRTH - 1)
    receives = (sends[1], sends[0], sends[3], sends[2])

    def each(side, there, act):
        @pl.when(there[side])
        def _():
            for k in sides[side]:
                act(halo(k))

    for side in (0, 1):
        each(side, sends, lambda copy: copy.start())
    for copy in own:
        copy.wait()
    for f in range(6):
        for s in range(CELLS_S):
            pack[0, f, 2 * s : 2 * s + 2, :] = cells[f, s, 0:2, :]
            pack[1, f, 2 * s : 2 * s + 2, :] = cells[f, s, 6:8, :]
    for side in (2, 3):
        each(side, sends, lambda copy: copy.start())
    owners.start()
    for copy in points:
        copy.start()
    for device in other_x:
        pl.semaphore_signal(row_sem, inc=1, device_id=device, device_id_type=MESH)
    for f in range(6):
        for s in range(CELLS_S):
            wide[f, s, 8:16, :] = cells[f, s]

    @pl.when(t == 0)
    def _():
        above[0] = jnp.zeros((6, 2, 8, CELLS_R), F32)

    @pl.when(t == STREAM - 1)
    def _():
        above[1] = jnp.zeros((6, 2, 8, CELLS_R), F32)

    @pl.when(g == 0)
    def _():
        edge[0] = jnp.zeros((6, 8, CELLS_R), F32)

    @pl.when(g == GIRTH - 1)
    def _():
        edge[1] = jnp.zeros((6, 8, CELLS_R), F32)

    sub8 = lax.broadcasted_iota(jnp.int32, (8, 128), 0)
    lane8 = lax.broadcasted_iota(jnp.int32, (8, 128), 1)

    def sector(s, carry):
        count, place = carry
        mine = jnp.where(owner[s] == g, 1, 0)
        here = (sub8 == s // 8) & (lane8 // WIDTH == lax.rem(s, 8))
        value = jnp.where(mine > 0, count * WIDTH, -AZIMUTHS) + lax.rem(lane8, WIDTH)
        return count + mine, jnp.where(here, value, place)

    owners.wait()
    _, place = lax.fori_loop(
        0, SECTORS, sector, (jnp.int32(0), jnp.full((8, 128), -AZIMUTHS, jnp.int32))
    )
    row = lax.broadcasted_iota(jnp.int32, (256, 128), 0)
    slot = jnp.where(row < 192, row, row - 64)
    for k in range(8):
        hit = slot == place[k : k + 1, :]
        choose[:, k * 128 : (k + 1) * 128] = jnp.where(hit, 1.0, 0.0).astype(BF16)

    for copy in points:
        copy.wait()
    cid = ids_v[...].reshape(PLANE, AZIMUTHS)
    stream_cell = lax.shift_right_logical(cid, 11)
    girth_cell = lax.shift_right_logical(cid, 8) & 7
    wall_cell = cid & 255
    stack = [wall_cell.astype(F32).astype(BF16), stream_cell.astype(F32).astype(BF16)]
    stack.append(girth_cell.astype(F32).astype(BF16))
    for i in range(3):
        stack.extend(parts_of(frac_v[:, i].reshape(PLANE, AZIMUTHS), 3))
    picked = lax.dot_general(
        jnp.concatenate(stack, axis=0), choose[...], (((1,), (1,)), ((), ())),
        preferred_element_type=F32,
    )
    part = [picked[32 * i : 32 * i + 32] for i in range(12)]
    cell_q, cell_s, cell_g = [point_tiles(part[i]) for i in range(3)]
    f_s, f_g, f_q = [
        point_tiles(part[3 + 3 * i] + part[4 + 3 * i] + part[5 + 3 * i]) for i in range(3)
    ]
    vec[0] = cell_s
    vec[1] = f_s
    vec[2] = cell_g
    vec[3] = f_g
    vec[4] = cell_q
    low_parts = parts_of(1.0 - f_q, 2)
    high_parts = parts_of(f_q, 2)
    vec[5] = low_parts[0].astype(F32)
    vec[6] = low_parts[1].astype(F32)
    vec[7] = high_parts[0].astype(F32)
    vec[8] = high_parts[1].astype(F32)

    chosen = jnp.dot(choose[...], ft[...], preferred_element_type=F32).astype(BF16)
    four[0:256, :] = chosen[:, 0:256]
    four[256:512, :] = chosen[:, 256:512]

    def weights(n, carry):
        def v(i):
            return vec[i, pl.ds(n, 1), :]

        q = lax.broadcasted_iota(jnp.int32, (CELLS_R, 256), 0).astype(F32)
        at_q = q == v(4)
        at_up = q == v(4) + 1.0
        high = jnp.where(at_q, v(5), jnp.where(at_up, v(7), 0.0)).astype(BF16)
        low = jnp.where(at_q, v(6), jnp.where(at_up, v(8), 0.0)).astype(BF16)
        cols = pl.ds(pl.multiple_of(n * 256, 256), 256)
        W[0:256, cols] = high
        W[256:512, cols] = low
        return carry

    lax.fori_loop(0, TILES, weights, 0, unroll=2)
    sendb[...] = jnp.zeros_like(sendb)

    pl.semaphore_wait(row_sem, 3)
    pl.semaphore_signal(plane_sem, inc=1, device_id=across, device_id_type=MESH)

    for side in range(4):
        each(side, receives, lambda copy: copy.wait_recv())

    def gather(i, s):
        return pltpu.make_async_remote_copy(
            src_ref=nv.at[0, s], dst_ref=nv.at[RING - i, s],
            send_sem=gs_sem.at[i * CELLS_S + s], recv_sem=gr_sem.at[i * CELLS_S + s],
            device_id=ring_peer(i), device_id_type=MESH,
        )

    for s in range(CELLS_S):
        for f in range(6):
            wide[f, s, 6:8, :] = edge[0, f, 2 * s : 2 * s + 2, :]
            wide[f, s, 16:18, :] = edge[1, f, 2 * s : 2 * s + 2, :]
        updated, strain = Layer(cells, above, wide, s).velocity()
        for c in range(3):
            nv[0, s, c] = updated[c]
        strain_v[s] = strain
        for i in (2, 1, 3):
            gather(i, s).start()
    for s in range(CELLS_S):
        turb[0, s], turb[1, s] = Layer(cells, above, wide, s).turbulence(strain_v[s])
    results = [
        pltpu.make_async_copy(nv.at[0, s], nv_o.at[:, s], out_sem.at[s]) for s in range(CELLS_S)
    ]
    results.append(pltpu.make_async_copy(turb.at[0], ne_o, out_sem.at[4]))
    results.append(pltpu.make_async_copy(turb.at[1], nr_o, out_sem.at[5]))
    for copy in results:
        copy.start()

    def load_blocks(first, count):
        value = jnp.concatenate(
            [nv[first + b].reshape(ROWS, CELLS_R) for b in range(count)], axis=0
        )
        high, low = parts_of(value, 2)
        start = 2 * first * ROWS
        lhs[start : start + count * ROWS, :] = high
        lhs[start + count * ROWS : start + 2 * count * ROWS, :] = low

    def layers(blocks, n, sums):
        first, count = blocks
        start, rows = 2 * first * ROWS, count * ROWS
        cols = pl.ds(pl.multiple_of(n * 256, 256), 256)
        both = jnp.dot(
            lhs[start : start + 2 * rows, :], W[0:256, cols], preferred_element_type=F32
        )
        fine = jnp.dot(lhs[start : start + rows, :], W[256:512, cols], preferred_element_type=F32)
        out = both[0:rows] + both[rows : 2 * rows] + fine
        cell = jnp.broadcast_to(vec[0, pl.ds(n, 1), :], (8, 256))
        up = jnp.broadcast_to(vec[1, pl.ds(n, 1), :], (8, 256))
        stay = 1.0 - up
        for b in range(count):
            base = ((y * RING + lax.rem(z + first + b, RING)) * CELLS_S).astype(F32)
            above_base = cell - base
            for s in range(CELLS_S):
                weight = jnp.where(
                    above_base == s, stay, jnp.where(above_base == s - 1, up, 0.0)
                )
                for c in range(3):
                    at = b * ROWS + s * 24 + c * 8
                    term = weight * out[at : at + 8]
                    sums[c] = term if sums[c] is None else sums[c] + term
        return sums

    load_blocks(0, 1)

    def first_pass(n, carry):
        sums = layers((0, 1), n, [None] * 3)
        for c in range(3):
            acc[c * TILES + n] = sums[c]
        return carry

    lax.fori_loop(0, TILES, first_pass, 0, unroll=12)

    for i in range(1, RING):
        for s in range(CELLS_S):
            gather(i, s).wait_recv()
    load_blocks(1, RING - 1)

    near = g // 8
    column = lax.rem(g, 8)

    def slot_of(i):
        return pl.ds(pl.multiple_of(i * 8, 8), 8)

    def post(turn, j):
        half = 1 - near if turn == 0 else near
        turned = column + j % 8
        turned = jnp.where(turned >= 8, turned - 8, turned)
        across = 1 - y if j >= 8 else y
        dev = (other_t if j >= 8 else t, half * 8 + turned)
        return pltpu.make_async_remote_copy(
            src_ref=sendb.at[slot_of(16 * turn + across * 8 + turned), :],
            dst_ref=recvb.at[pl.ds(8 * (16 * turn + j), 8), :],
            send_sem=as_sem.at[turn], recv_sem=ar_sem.at[turn],
            device_id=dev, device_id_type=MESH,
        )

    def posts(turn):
        span = pl.ds(128 * turn + 8 * turn, 128 - 8 * turn)
        return pltpu.make_async_remote_copy(
            src_ref=sendb.at[span, :], dst_ref=recvb.at[span, :],
            send_sem=as_sem.at[turn], recv_sem=ar_sem.at[turn],
            device_id=plane_peer(True, 0), device_id_type=MESH,
        )

    pl.semaphore_wait(plane_sem, 1)
    for turn in range(2):
        offset = ((1 - near) if turn == 0 else near) * HALF

        def second_pass(k, carry, offset=offset):
            n = offset + k
            sums = layers((1, 3), n, [acc[c * TILES + n] for c in range(3)])
            cell = vec[2, pl.ds(n, 1), :]
            up = vec[3, pl.ds(n, 1), :]
            side = lax.broadcasted_iota(jnp.int32, (8, 256), 0).astype(F32)
            weight = jnp.where(side == cell, 1.0 - up, jnp.where(side == cell + 1.0, up, 0.0))
            for c in range(3):
                disk[pl.ds(c * 16 + k, 1), :] = jnp.sum(sums[c] * weight, axis=0, keepdims=True)
            return carry

        lax.fori_loop(0, HALF, second_pass, 0, unroll=12)
        rows = jnp.concatenate(
            [radius_rows(disk[c * 16 : c * 16 + HALF, :]) for c in range(3)], axis=0
        )
        high, low = parts_of(rows, 2)
        both = jnp.dot(
            jnp.concatenate([high, low], axis=0), four[0:256, :], preferred_element_type=F32
        )
        fine = jnp.dot(high, four[256:512, :], preferred_element_type=F32)
        spectrum = both[0:48] + both[48:96] + fine
        for c in range(3):
            for k in range(2):
                sendb[pl.ds(128 * turn + 2 * c + k, 16, stride=8), :] = spectrum[
                    c * 16 : (c + 1) * 16, k * 128 : (k + 1) * 128
                ]

        for j in range(15, turn - 1, -1):
            post(turn, j).start()

    mine = pltpu.make_async_copy(
        sendb.at[slot_of(16 + y * 8 + column), :], recvb.at[pl.ds(128, 8), :], out_sem.at[6]
    )
    mine.start()
    results.append(mine)
    for side in range(4):
        each(side, sends, lambda copy: copy.wait_send())
    for i in range(1, RING):
        for s in range(CELLS_S):
            gather(i, s).wait_send()
    for copy in results:
        copy.wait()
    for turn in range(2):
        posts(turn).wait_send()
        posts(turn).wait_recv()


def place_results(nv, ne, nr, parts, nv_o, ne_o, nr_o, harm_o):
    nv_o[...] = nv[...]
    ne_o[...] = ne[...]
    nr_o[...] = nr[...]
    total = jnp.sum(parts[...].reshape(PLANE, 8, 128), axis=0)
    for k in range(6):
        harm_o[0:1, k * 128 : (k + 1) * 128] = total[k : k + 1, :]


def body(velocity, pressure, kinetic_energy, dissipation_rate, corner_ids, fractions, sector_owner):
    hbm = pl.BlockSpec(memory_space=pltpu.HBM)
    vmem = pl.BlockSpec(memory_space=pltpu.VMEM)
    dma = pltpu.SemaphoreType.DMA
    shapes = (
        jax.ShapeDtypeStruct(velocity.shape, F32),
        jax.ShapeDtypeStruct(pressure.shape, F32),
        jax.ShapeDtypeStruct(pressure.shape, F32),
        jax.ShapeDtypeStruct((1, 6 * MODES), F32),
    )
    results = pl.pallas_call(
        kernel,
        out_shape=shapes[:3] + (jax.ShapeDtypeStruct((PLANE * 8, 128), F32),),
        in_specs=[hbm] * 8,
        out_specs=(hbm,) * 4,
        scratch_shapes=[
            pltpu.SMEM((SECTORS,), jnp.int32),
            pltpu.VMEM((6, CELLS_S, CELLS_G, CELLS_R), F32),
            pltpu.VMEM((2, 6, 2, CELLS_G, CELLS_R), F32),
            pltpu.VMEM((6, CELLS_S, 24, CELLS_R), F32),
            pltpu.VMEM((2, 6, 8, CELLS_R), F32),
            pltpu.VMEM((2, 6, 8, CELLS_R), F32),
            pltpu.VMEM((RING, CELLS_S, 3, CELLS_G, CELLS_R), F32),
            pltpu.VMEM((CELLS_S, CELLS_G, CELLS_R), F32),
            pltpu.VMEM((2, CELLS_S, CELLS_G, CELLS_R), F32),
            pltpu.VMEM((2, GIRTH, AZIMUTHS), jnp.int32),
            pltpu.VMEM((2, 3, GIRTH, AZIMUTHS), F32),
            pltpu.VMEM((AZIMUTHS, 512), BF16),
            pltpu.VMEM((256, AZIMUTHS), BF16),
            pltpu.VMEM((512, TILES * 256), BF16),
            pltpu.VMEM((2 * RING * ROWS, 256), BF16),
            pltpu.VMEM((9, TILES, 256), F32),
            pltpu.VMEM((3 * TILES, 8, 256), F32),
            pltpu.VMEM((48, 256), F32),
            pltpu.VMEM((512, 256), BF16),
            pltpu.VMEM((PLANE * 8, 128), F32),
            dma((10,)),
            dma((7,)),
            dma((10,)),
            dma((10,)),
            dma((RING * CELLS_S,)),
            dma((RING * CELLS_S,)),
            dma((2,)),
            dma((2,)),
            pltpu.SemaphoreType.REGULAR,
            pltpu.SemaphoreType.REGULAR,
        ],
        compiler_params=pltpu.CompilerParams(
            collective_id=0, has_side_effects=True, vmem_limit_bytes=VMEM_BYTES
        ),
    )(
        velocity, pressure, kinetic_energy, dissipation_rate, corner_ids, fractions,
        sector_owner.reshape(SECTORS), jnp.asarray(fourier_parts()),
    )
    return pl.pallas_call(
        place_results,
        out_shape=shapes,
        in_specs=[vmem] * 4,
        out_specs=(vmem,) * 4,
        compiler_params=pltpu.CompilerParams(vmem_limit_bytes=VMEM_BYTES),
    )(*results)


def solution(mesh):
    return jax.shard_map(
        body,
        mesh=mesh,
        in_specs=(
            P(None, "stream", "girth", None),
            P("stream", "girth", None),
            P("stream", "girth", None),
            P("stream", "girth", None),
            P(),
            P(),
            P(),
        ),
        out_specs=(
            P(None, "stream", "girth", None),
            P("stream", "girth", None),
            P("stream", "girth", None),
            P(("stream", "girth"), None),
        ),
        check_vma=False,
    )
```
